256 devices in a mesh: dp: 16 (over z, x_hi), ctx: 16 (over x_lo, y, core).
Axes of the slice: x: 4 (x_hi: 2, x_lo: 2; x = x_hi * 2 + x_lo), y: 4, z: 8, core: 2. Of those that a mesh axis runs over, the one named last changes fastest.
Arguments:
- features: bfloat16 [16, 8192, 768], P('dp', 'ctx'), may hold values from -24 to 24
- bases: int32 [16, 8192], P('dp', 'ctx'), may hold values from 0 to 3
- dna_table: bfloat16 [4, 768], replicated, may hold values from -6 to 6
- norm_gain: bfloat16 [768], replicated, may hold values from 0.099609375 to 1.8984375
- w_conv: bfloat16 [5, 768, 768], replicated, may hold values from -0.09375 to 0.09375
- w_query: bfloat16 [768, 768], replicated, may hold values from -0.21875 to 0.21875
- w_key: bfloat16 [768, 768], replicated, may hold values from -0.21875 to 0.21875
- w_value: bfloat16 [768, 768], replicated, may hold values from -0.21875 to 0.21875
- w_out: bfloat16 [768, 768], replicated, may hold values from -0.21875 to 0.21875
- cotangent: bfloat16 [16, 512, 768], P('dp', 'ctx'), may hold values from -48 to 48
Outputs:
- grad_features: bfloat16 [16, 8192, 768], P('dp', 'ctx')
- grad_conv: float32 [768, 5, 768], P('ctx', None, 'dp')
The draws below stay inside these ranges and needn't reach their ends.
All inputs are finite; a program needn't handle non-finite values.
Results may differ from the reference program's by a relative error of at most 0.025.
The reference program's roundings to bfloat16 on the way count: a program that leaves them out, or rounds other values in their place, can miss the bound.
Values may be sent and summed in bfloat16 or wider, within the bound.
A program may use at most 128 MiB of HBM per device.

```python
import jax
import jax.numpy as jnp
from jax import lax

C = 768
HEADS = 6
DH = 128
KW = 5
POOL = 16
LEN = 8192
TOKENS = 512
SEGS = 16


def draw_features(key, part):
    rough_key = jax.random.fold_in(jax.random.fold_in(key, 11), 0)
    blocks = LEN // POOL
    values = jax.random.normal(rough_key, (SEGS, blocks, POOL, C), jnp.float32)
    return jnp.clip(values.reshape(SEGS, LEN, C), -24.0, 24.0).astype(jnp.bfloat16)


def with_ends(array, rng, least, largest):
    index_at = [jax.random.randint(jax.random.fold_in(rng, axis), (), 0, length) for axis, length in enumerate(array.shape)]
    longest = array.shape.index(max(array.shape))
    beside = index_at[:longest] + [(index_at[longest] + 1) % array.shape[longest]] + index_at[longest + 1:]
    return array.at[tuple(index_at)].set(least).at[tuple(beside)].set(largest)


def shard_levels(stream_key, extent, pieces, low, largest):
    factor_of, own = 1.0, jax.random.fold_in(stream_key, 6)
    for position, blocks in pieces:
        steps = jnp.exp(jax.random.uniform(jax.random.fold_in(own, position), (blocks,), jnp.float32, low / len(pieces), largest / len(pieces)))
        factor_of = factor_of * jnp.repeat(steps, extent[position] // blocks).reshape([-1 if axis == position else 1 for axis in range(len(extent))])
    return factor_of


def noise(own_key, shape, deviation, bound, cuts=(), kind=jnp.bfloat16):
    loudness = shard_levels(own_key, shape, cuts, -0.22, 0.18) if cuts else 1.0
    entries = jax.random.normal(own_key, shape, jnp.float32) * deviation * loudness
    return jnp.minimum(jnp.maximum(entries, -bound), bound).astype(kind)


def setup_inputs(seed: int = 0) -> dict:
    key_of = jax.random.split(jax.random.key(seed), 11)
    return {
        "features": draw_features(jax.random.fold_in(key_of[10], 71), 0),
        "bases": with_ends(jax.random.randint(key_of[1], (SEGS, LEN), 0, 4), jax.random.fold_in(key_of[1], 1), 0, 3).astype(jnp.int32),
        "dna_table": noise(key_of[2], (4, C), 1.0, 6.0),
        "norm_gain": jnp.clip(1.0 + 0.18 * jax.random.normal(key_of[3], (C,), jnp.float32), 0.099609375, 1.8984375).astype(jnp.bfloat16),
        "w_conv": noise(key_of[4], (KW, C, C), (KW * C) ** -0.5, 0.09375),
        "w_query": noise(key_of[5], (C, C), C ** -0.5, 0.21875),
        "w_key": noise(key_of[6], (C, C), C ** -0.5, 0.21875),
        "w_value": noise(key_of[7], (C, C), C ** -0.5, 0.21875),
        "w_out": noise(key_of[8], (C, C), C ** -0.5, 0.21875),
        "cotangent": noise(key_of[9], (SEGS, TOKENS, C), 8.0, 48.0, ((0, 16), (1, 16))),
    }


EPSILON = 1e-06
GELU_SCALE = 0.7978845608028654
CUBIC = 0.044715

def gelu_pair(inputs):
    inner = GELU_SCALE * (inputs + CUBIC * inputs ** 3)
    tanh_val = jnp.tanh(inner)
    values = 0.5 * inputs * (1.0 + tanh_val)
    slopes = 0.5 * (1.0 + tanh_val) + 0.5 * inputs * (1.0 - tanh_val ** 2) * GELU_SCALE * (1.0 + 3.0 * CUBIC * inputs ** 2)
    return (values, slopes)

def heads_split(matrix):
    return matrix.reshape(matrix.shape[0], HEADS, DH).astype(jnp.float32)

def dot_right_t(left, right):
    return lax.dot_general(left, right, (((1,), (1,)), ((), ())), preferred_element_type=jnp.float32)

def dot_left_t(left, right):
    return lax.dot_general(left, right, (((0,), (0,)), ((), ())), preferred_element_type=jnp.float32)

def segment(seg_feat, seg_base, seg_cot, dna_table, norm_gain, w_conv, w_query, w_key, w_value, w_out):
    half_width = KW // 2
    onehot = (seg_base[:, None] == jnp.arange(4, dtype=jnp.int32)[None, :]).astype(jnp.bfloat16)
    summed_in = seg_feat.astype(jnp.float32) + jnp.dot(onehot, dna_table, preferred_element_type=jnp.float32)
    inv_rms = lax.rsqrt(lax.optimization_barrier(jnp.mean(summed_in * summed_in, axis=-1, keepdims=True)) + EPSILON)
    normed = summed_in * inv_rms
    gain_f = norm_gain.astype(jnp.float32)
    pre_gelu = normed * gain_f
    gelu_val, slopes = gelu_pair(pre_gelu)
    act = gelu_val.astype(jnp.bfloat16)
    length = act.shape[0]
    padded = jnp.pad(act, ((half_width, half_width), (0, 0)))
    conv = jnp.zeros((length, C), jnp.float32)
    for offset in range(KW):
        conv = conv + jnp.dot(padded[offset:offset + length], w_conv[offset], preferred_element_type=jnp.float32)
    resid = summed_in + conv
    pooled = resid.reshape(-1, POOL, C).mean(axis=1).astype(jnp.bfloat16)
    queries = jnp.dot(pooled, w_query, preferred_element_type=jnp.float32).astype(jnp.bfloat16)
    keys_all = jnp.dot(pooled, w_key, preferred_element_type=jnp.float32).astype(jnp.bfloat16)
    values_all = jnp.dot(pooled, w_value, preferred_element_type=jnp.float32).astype(jnp.bfloat16)
    scale = 1.0 / DH ** 0.5
    scores = jnp.einsum('qhd,khd->hqk', heads_split(queries), heads_split(keys_all)) * scale
    probs = jax.nn.softmax(scores, axis=-1)
    probs_b = probs.astype(jnp.bfloat16)
    attn_out = jnp.einsum('hqk,khd->qhd', probs_b.astype(jnp.float32), heads_split(values_all))
    attn_out = attn_out.reshape(-1, C).astype(jnp.bfloat16)
    grad_attn = dot_right_t(seg_cot, w_out).astype(jnp.bfloat16)
    grad_prob = jnp.einsum('qhd,khd->hqk', heads_split(grad_attn), heads_split(values_all))
    row_delta = lax.optimization_barrier(jnp.sum(heads_split(grad_attn) * heads_split(attn_out), axis=-1)).transpose(1, 0)[:, :, None]
    grad_score = (probs * (grad_prob - row_delta) * scale).astype(jnp.bfloat16).astype(jnp.float32)
    grad_q = jnp.einsum('hqk,khd->qhd', grad_score, heads_split(keys_all)).reshape(-1, C).astype(jnp.bfloat16)
    grad_k = jnp.einsum('hqk,qhd->khd', grad_score, heads_split(queries)).reshape(-1, C).astype(jnp.bfloat16)
    grad_v = jnp.einsum('hqk,qhd->khd', probs_b.astype(jnp.float32), heads_split(grad_attn)).reshape(-1, C).astype(jnp.bfloat16)
    grad_pooled = seg_cot.astype(jnp.float32) + dot_right_t(grad_q, w_query) + dot_right_t(grad_k, w_key) + dot_right_t(grad_v, w_value)
    grad_rows = jnp.repeat((grad_pooled / POOL).astype(jnp.bfloat16), POOL, axis=0)
    grad_pad = jnp.pad(grad_rows, ((half_width, half_width), (0, 0)))
    grad_act = jnp.zeros((length, C), jnp.float32)
    wgrad_list = []
    for offset in range(KW):
        begin = 2 * half_width - offset
        grad_act = grad_act + dot_right_t(grad_pad[begin:begin + length], w_conv[offset])
        wgrad_list.append(dot_left_t(padded[offset:offset + length], grad_rows))
    wgrad = jnp.stack(wgrad_list, axis=1)
    grad_norm = grad_act * slopes * gain_f
    grad_in = grad_rows.astype(jnp.float32) + inv_rms * (grad_norm - normed * lax.optimization_barrier(jnp.mean(grad_norm * normed, axis=-1, keepdims=True)))
    return (grad_in.astype(jnp.bfloat16), wgrad)

def reference(features, bases, dna_table, norm_gain, w_conv, w_query, w_key, w_value, w_out, cotangent):

    def segment_step(totals, slices):
        seg_feat, seg_base, seg_cot = slices
        grad_in, wgrad = segment(seg_feat, seg_base, seg_cot, dna_table, norm_gain, w_conv, w_query, w_key, w_value, w_out)
        return (totals + wgrad, grad_in)
    totals, grad_list = lax.scan(segment_step, jnp.zeros((C, KW, C), jnp.float32), (features, bases, cotangent))
    factor = 1.0 / (SEGS * LEN) ** 0.5
    return (grad_list, totals * factor)
```

```python
import functools

import jax
import jax.numpy as jnp
from jax import lax
from jax.experimental import pallas as pl
from jax.experimental.pallas import tpu as pltpu
from jax.sharding import PartitionSpec as P

HEADS = 6
DH = 128
C = 768
KW = 5
POOL = 16
ROWS = 512
TOK = 32
SEG_TOK = 512
CTX = 16
NZ = 8
PLANE = 32
BLK = 48
HALF = 384
XW = 256
EPSILON = 1e-06
GELU_SCALE = 0.7978845608028654
CUBIC = 0.044715
MESH = pl.DeviceIdType.MESH
F32 = jnp.float32
BF16 = jnp.bfloat16


def dot(a, b):
    return jnp.dot(a, b, preferred_element_type=F32)


def dot_rt(a, b):
    return lax.dot_general(a, b, (((1,), (1,)), ((), ())), preferred_element_type=F32)


def window_matrix(first, columns):
    row = lax.broadcasted_iota(jnp.int32, (KW * TOK, columns), 0)
    low = (row % TOK) * POOL + row // TOK - 2
    place = lax.broadcasted_iota(jnp.int32, (KW * TOK, columns), 1) + first
    return jnp.where((place >= low) & (place < low + POOL), 1.0, 0.0).astype(BF16)


def body(
    feat_h, base_h, table_h, gain_h, wc_h, wq_h, wk_h, wv_h, wo_h, cot_h,
    grad_in_ref, grad_conv_ref,
    feat, base, table, gain, wc, wq, wk, wv, wo, cot,
    emb, act, normed, inv, slope, win, halo, xs, xr, xt,
    qs, hb, pt, gst, go, gb, grp, grr, grh, grs, rs, rr, edge,
    in_sem, send_sem, recv_sem,
):
    dp = lax.axis_index("dp")
    ctx = lax.axis_index("ctx")
    zz = dp // 2
    hi = dp % 2
    me = hi * CTX + ctx

    def plane_id(p):
        return {"dp": zz * 2 + p // CTX, "ctx": p % CTX}

    def z_id(z):
        return {"dp": z * 2 + hi, "ctx": ctx}

    pairs = [
        (base_h, base), (table_h, table), (gain_h, gain), (feat_h, feat), (cot_h, cot), (wo_h, wo),
        (wc_h, wc), (wq_h, wq), (wk_h, wk), (wv_h, wv),
    ]
    loads = [pltpu.make_async_copy(s, d, in_sem.at[i]) for i, (s, d) in enumerate(pairs)]
    for load in loads:
        load.start()

    barrier = pltpu.get_barrier_semaphore()

    @pl.loop(1, PLANE)
    def _(i):
        pl.semaphore_signal(barrier, inc=1, device_id=plane_id((me + i) % PLANE), device_id_type=MESH)

    @pl.loop(1, NZ)
    def _(i):
        pl.semaphore_signal(barrier, inc=1, device_id=z_id((zz + i) % NZ), device_id_type=MESH)

    win[...] = window_matrix(0, ROWS)
    for load in loads[:4]:
        load.wait()

    base_col = jnp.broadcast_to(base[...], (128, ROWS)).T
    onehot = jnp.where(
        base_col == lax.broadcasted_iota(jnp.int32, (ROWS, 128), 1), 1.0, 0.0
    ).astype(BF16)
    row_id = lax.broadcasted_iota(jnp.int32, (128, C), 0)
    tab = jnp.zeros((128, C), F32)
    for b in range(4):
        tab = jnp.where(row_id == b, table[b : b + 1, :].astype(F32), tab)
    tab = tab.astype(BF16)
    emb[...] = dot(onehot, tab).astype(BF16)
    gain_f = gain[...].astype(F32)

    def rows_forward(r0):
        rows = pl.ds(r0, POOL)
        s = feat[rows, :].astype(F32) + emb[rows, :].astype(F32)
        scale = lax.rsqrt(jnp.mean(s * s, axis=-1, keepdims=True) + EPSILON)
        n = s * scale
        u = n * gain_f
        t = jnp.tanh(GELU_SCALE * (u + CUBIC * (u * u * u)))
        act[rows, :] = (0.5 * u * (1.0 + t)).astype(BF16)
        normed[rows, :] = n
        inv[rows, :] = scale

    rows_forward(0)
    rows_forward(ROWS - POOL)
    pl.semaphore_wait(barrier, PLANE - 1 + NZ - 1)

    def sides(first, last, into, sem):
        low = pltpu.make_async_remote_copy(
            src_ref=first, dst_ref=into.at[1], send_sem=send_sem.at[sem], recv_sem=recv_sem.at[sem],
            device_id={"dp": dp, "ctx": jnp.maximum(ctx - 1, 0)}, device_id_type=MESH,
        )
        high = pltpu.make_async_remote_copy(
            src_ref=last, dst_ref=into.at[0], send_sem=send_sem.at[sem + 1], recv_sem=recv_sem.at[sem + 1],
            device_id={"dp": dp, "ctx": jnp.minimum(ctx + 1, CTX - 1)}, device_id_type=MESH,
        )

        @pl.when(ctx > 0)
        def _():
            low.start()

        @pl.when(ctx < CTX - 1)
        def _():
            high.start()

        @pl.when(ctx == 0)
        def _():
            into[0] = jnp.zeros((16, C), BF16)

        @pl.when(ctx == CTX - 1)
        def _():
            into[1] = jnp.zeros((16, C), BF16)

        return low, high

    def sides_arrive(copies):
        low, high = copies

        @pl.when(ctx < CTX - 1)
        def _():
            low.wait_recv()

        @pl.when(ctx > 0)
        def _():
            high.wait_recv()

    def sides_sent(copies):
        low, high = copies

        @pl.when(ctx > 0)
        def _():
            low.wait_send()

        @pl.when(ctx < CTX - 1)
        def _():
            high.wait_send()

    act_sides = sides(act.at[pl.ds(0, 16), :], act.at[pl.ds(ROWS - 16, 16), :], halo, 0)

    @pl.loop(1, ROWS // POOL - 1)
    def _(i):
        rows_forward(pl.multiple_of(i * POOL, POOL))

    sums = dot(win[...], act[...])
    mean_rows = win[2 * TOK : 3 * TOK, :]
    counts = dot(mean_rows, onehot).astype(BF16)
    pooled_in = dot(mean_rows, feat[...]) + dot(counts, tab)

    loads[4].wait()
    loads[5].wait()
    grad_attn = dot_rt(cot[...], wo[...]).astype(BF16)
    for h in range(HEADS):
        qs[h, 3] = grad_attn[:, h * DH : (h + 1) * DH]

    sides_arrive(act_sides)
    edge_win = jnp.concatenate([window_matrix(-16, 16), window_matrix(ROWS, 16)], axis=1)
    sums = sums + dot(edge_win, jnp.concatenate([halo[0], halo[1]], axis=0))
    high_part = sums.astype(BF16)
    low_part = (sums - high_part.astype(F32)).astype(BF16)

    loads[6].wait()
    conv = jnp.zeros((2 * TOK, C), F32)
    for j in range(KW):
        part = slice(j * TOK, (j + 1) * TOK)
        conv = conv + dot(jnp.concatenate([high_part[part], low_part[part]], axis=0), wc[j])
    pooled = ((pooled_in + conv[:TOK] + conv[TOK:]) * (1.0 / POOL)).astype(BF16)

    for i in range(7, 10):
        loads[i].wait()
    for k, weight in enumerate((wq, wk, wv)):
        made = dot(pooled, weight[...]).astype(BF16)
        for h in range(HEADS):
            qs[h, k] = made[:, h * DH : (h + 1) * DH]

    def to_head(h):
        return pltpu.make_async_remote_copy(
            src_ref=qs.at[h], dst_ref=hb.at[:, pl.ds(pl.multiple_of(ctx * TOK, TOK), TOK), :],
            send_sem=send_sem.at[4 + h], recv_sem=recv_sem.at[4],
            device_id={"dp": dp, "ctx": 2 * h}, device_id_type=MESH,
        )

    for h in range(HEADS):
        @pl.when(ctx != 2 * h)
        def _():
            to_head(h).start()

    for c in range(CTX):
        cols = [sums[j * TOK : (j + 1) * TOK, c * BLK : (c + 1) * BLK] for j in range(KW)]
        cols.append(jnp.zeros((TOK, XW - KW * BLK), F32))
        xs[c] = jnp.concatenate(cols, axis=1).astype(BF16)

    @pl.loop(1, PLANE)
    def _(i):
        p = (me + i) % PLANE
        pltpu.make_async_remote_copy(
            src_ref=xs.at[p % CTX], dst_ref=xr.at[me], send_sem=send_sem.at[10], recv_sem=recv_sem.at[5],
            device_id=plane_id(p), device_id_type=MESH,
        ).start()

    xr[me] = xs[ctx]

    head = ctx // 2
    is_head = (ctx % 2 == 0) & (ctx < 2 * HEADS)

    def from_head(c):
        return pltpu.make_async_remote_copy(
            src_ref=go.at[:, pl.ds(pl.multiple_of(c * TOK, TOK), TOK), :], dst_ref=gb.at[head],
            send_sem=send_sem.at[11], recv_sem=recv_sem.at[6],
            device_id={"dp": dp, "ctx": c}, device_id_type=MESH,
        )

    @pl.when(is_head)
    def _():
        hb[:, pl.ds(pl.multiple_of(ctx * TOK, TOK), TOK), :] = qs[head]
        arrived = hb.at[:, pl.ds(0, SEG_TOK - TOK), :]
        pltpu.make_async_copy(arrived, arrived, recv_sem.at[4]).wait()
        scale = 1.0 / DH**0.5
        keys = hb[1]
        values = hb[2]
        values_t = values.T

        @pl.loop(0, SEG_TOK // 128)
        def _(i):
            part = pl.ds(pl.multiple_of(i * 128, 128), 128)
            query = hb[0, part, :]
            grad = hb[3, part, :]
            score = dot_rt(keys, query) * scale
            expo = jnp.exp(score - jnp.max(score, axis=0, keepdims=True))
            prob = expo * (1.0 / jnp.sum(expo, axis=0, keepdims=True))
            prob_b = prob.astype(BF16)
            out_t = dot(values_t, prob_b).astype(BF16).astype(F32)
            delta = jnp.sum(grad.T.astype(F32) * out_t, axis=0, keepdims=True)
            grad_prob = dot_rt(values, grad)
            pt[:, part] = prob_b
            gst[:, part] = (prob * (grad_prob - delta) * scale).astype(BF16)

        go[0] = dot(keys.T, gst[...]).T.astype(BF16)
        go[1] = dot(gst[...], hb[0]).astype(BF16)
        go[2] = dot(pt[...], hb[3]).astype(BF16)

        @pl.loop(1, CTX)
        def _(i):
            from_head((ctx + i) % CTX).start()

        gb[head] = go[:, pl.ds(pl.multiple_of(ctx * TOK, TOK), TOK), :]
        five = gb.at[pl.ds(0, HEADS - 1)]
        pltpu.make_async_copy(five, five, recv_sem.at[6]).wait()

    @pl.when(jnp.logical_not(is_head))
    def _():
        pltpu.make_async_copy(gb, gb, recv_sem.at[6]).wait()

    grad_pooled = cot[...].astype(F32)
    for k, weight in enumerate((wq, wk, wv)):
        whole = jnp.concatenate([gb[h, k] for h in range(HEADS)], axis=1)
        grad_pooled = grad_pooled + dot_rt(whole, weight[...])
    grad_f = (grad_pooled * (1.0 / POOL)).astype(BF16).astype(F32)
    grs[...] = grad_f.astype(BF16)
    for h in range(2):
        cols = [grad_f[:, (2 * z + h) * BLK : (2 * z + h + 1) * BLK] for z in range(NZ)]
        grp[h] = jnp.concatenate(cols, axis=1).astype(BF16)

    @pl.loop(1, PLANE)
    def _(i):
        p = (me + i) % PLANE
        pltpu.make_async_remote_copy(
            src_ref=grp.at[p // CTX], dst_ref=grr.at[me], send_sem=send_sem.at[12], recv_sem=recv_sem.at[7],
            device_id=plane_id(p), device_id_type=MESH,
        ).start()

    grr[me] = grp[hi]
    row_sides = sides(grs.at[pl.ds(0, 16), :], grs.at[pl.ds(16, 16), :], grh, 2)

    @pl.loop(0, ROWS // POOL)
    def _(i):
        rows = pl.ds(pl.multiple_of(i * POOL, POOL), POOL)
        u = normed[rows, :] * gain_f
        square = u * u
        t = jnp.tanh(GELU_SCALE * (u + CUBIC * (square * u)))
        d = 0.5 * (1.0 + t) + 0.5 * u * (1.0 - t * t) * GELU_SCALE * (1.0 + 3.0 * CUBIC * square)
        slope[rows, :] = d * gain_f

    others = xr.at[pl.ds(0, PLANE - 1)]
    pltpu.make_async_copy(others, others, recv_sem.at[5]).wait()
    for i in range(PLANE * TOK // 128):
        block = jnp.concatenate([xr[4 * i + k] for k in range(4)], axis=0)
        xt[:, i * 128 : (i + 1) * 128] = block.T

    others = grr.at[pl.ds(0, PLANE - 1)]
    pltpu.make_async_copy(others, others, recv_sem.at[7]).wait()
    factor = 1.0 / (CTX * CTX * ROWS) ** 0.5
    made = dot(xt[...], grr[...].reshape(PLANE * TOK, HALF)) * factor
    rs[...] = made.T.astype(BF16)

    @pl.loop(1, NZ)
    def _(i):
        z = (zz + i) % NZ
        pltpu.make_async_remote_copy(
            src_ref=rs.at[pl.ds(pl.multiple_of(z * BLK, 16), BLK), :], dst_ref=rr.at[zz],
            send_sem=send_sem.at[13], recv_sem=recv_sem.at[8],
            device_id=z_id(z), device_id_type=MESH,
        ).start()

    rr[zz] = rs[pl.ds(pl.multiple_of(zz * BLK, 16), BLK), :]

    sides_arrive(row_sides)
    ext = jnp.concatenate([grh[0], grs[...], grh[1]], axis=0)
    first0 = first1 = mid = last0 = last1 = None
    for j in range(KW):
        y = dot_rt(ext, wc[j])
        own, before, after = y[16:48], y[15:47], y[17:49]
        terms = (
            before if j >= 3 else own,
            before if j >= 4 else own,
            own,
            after if j < 1 else own,
            after if j < 2 else own,
        )
        if j == 0:
            first0, first1, mid, last0, last1 = terms
        else:
            first0, first1, mid, last0, last1 = (
                a + b for a, b in zip((first0, first1, mid, last0, last1), terms)
            )
    for k, value in enumerate((first0, first1, mid, last0, last1, grs[...].astype(F32))):
        edge[k] = value

    in_group = lax.broadcasted_iota(jnp.int32, (POOL, C), 0)

    @pl.loop(0, TOK)
    def _(i):
        rows = pl.ds(pl.multiple_of(i * POOL, POOL), POOL)
        one = pl.ds(i, 1)
        g = jnp.broadcast_to(edge[2, one, :], (POOL, C))
        for r, k in ((0, 0), (1, 1), (14, 3), (15, 4)):
            g = jnp.where(in_group == r, edge[k, one, :], g)
        g = g * slope[rows, :]
        n = normed[rows, :]
        mean = jnp.mean(g * n, axis=-1, keepdims=True)
        grad_in_ref[rows, :] = (edge[5, one, :] + inv[rows, :] * (g - n * mean)).astype(BF16)

    others = rr.at[pl.ds(0, NZ - 1)]
    pltpu.make_async_copy(others, others, recv_sem.at[8]).wait()
    total = rr[0].astype(F32)
    for z in range(1, NZ):
        total = total + rr[z].astype(F32)
    grad_conv_ref[...] = total

    sides_sent(act_sides)
    sides_sent(row_sides)
    for h in range(HEADS):
        @pl.when(ctx != 2 * h)
        def _():
            to_head(h).wait_send()
    part = xr.at[pl.ds(0, PLANE - 1)]
    pltpu.make_async_copy(part, part, send_sem.at[10]).wait()

    @pl.when(is_head)
    def _():
        part = go.at[:, pl.ds(0, SEG_TOK - TOK), :]
        pltpu.make_async_copy(part, part, send_sem.at[11]).wait()

    part = grr.at[pl.ds(0, PLANE - 1)]
    pltpu.make_async_copy(part, part, send_sem.at[12]).wait()
    part = rr.at[pl.ds(0, NZ - 1)]
    pltpu.make_async_copy(part, part, send_sem.at[13]).wait()


def per_device(
    features, bases, dna_table, norm_gain, w_conv, w_query, w_key, w_value, w_out, cotangent
):
    vmem = pltpu.VMEM
    scratch = [
        vmem((ROWS, C), BF16), vmem((1, ROWS), jnp.int32), vmem((4, C), BF16), vmem((1, C), BF16),
        vmem((KW, C, C), BF16), vmem((C, C), BF16), vmem((C, C), BF16), vmem((C, C), BF16),
        vmem((C, C), BF16), vmem((TOK, C), BF16),
        vmem((ROWS, C), BF16),
        vmem((ROWS, C), BF16),
        vmem((ROWS, C), F32),
        vmem((ROWS, 1), F32),
        vmem((ROWS, C), F32),
        vmem((KW * TOK, ROWS), BF16),
        vmem((2, 16, C), BF16),
        vmem((CTX, TOK, XW), BF16),
        vmem((PLANE, TOK, XW), BF16),
        vmem((XW, PLANE * TOK), BF16),
        vmem((HEADS, 4, TOK, DH), BF16),
        vmem((4, SEG_TOK, DH), BF16),
        vmem((SEG_TOK, SEG_TOK), BF16),
        vmem((SEG_TOK, SEG_TOK), BF16),
        vmem((3, SEG_TOK, DH), BF16),
        vmem((HEADS, 3, TOK, DH), BF16),
        vmem((2, TOK, HALF), BF16),
        vmem((PLANE, TOK, HALF), BF16),
        vmem((2, 16, C), BF16),
        vmem((TOK, C), BF16),
        vmem((HALF, XW), BF16),
        vmem((NZ, BLK, XW), BF16),
        vmem((6, TOK, C), F32),
        pltpu.SemaphoreType.DMA((10,)),
        pltpu.SemaphoreType.DMA((14,)),
        pltpu.SemaphoreType.DMA((9,)),
    ]
    grad_in, grad_conv = pl.pallas_call(
        body,
        out_shape=(
            jax.ShapeDtypeStruct((ROWS, C), BF16),
            jax.ShapeDtypeStruct((BLK, XW), F32),
        ),
        in_specs=[pl.BlockSpec(memory_space=pl.ANY)] * 10,
        out_specs=(pl.BlockSpec(memory_space=pltpu.VMEM),) * 2,
        scratch_shapes=scratch,
        compiler_params=pltpu.CompilerParams(
            collective_id=0, has_side_effects=True, vmem_limit_bytes=48 * 1024 * 1024
        ),
        cost_estimate=pl.CostEstimate(flops=10**9, bytes_accessed=12 * 10**6, transcendentals=10**6),
    )(
        features[0], bases, dna_table, norm_gain[None], w_conv, w_query, w_key, w_value, w_out,
        cotangent[0],
    )
    grad_conv = grad_conv[:, : KW * BLK].reshape(BLK, KW, BLK).transpose(2, 1, 0)
    return grad_in[None], grad_conv


def solution(mesh):
    in_specs = (
        P("dp", "ctx", None),
        P("dp", "ctx"),
        P(),
        P(),
        P(),
        P(),
        P(),
        P(),
        P(),
        P("dp", "ctx", None),
    )
    out_specs = (P("dp", "ctx", None), P("ctx", None, "dp"))
    return jax.shard_map(
        per_device, mesh=mesh, in_specs=in_specs, out_specs=out_specs, check_vma=False
    )
```

```python
import functools

import jax
import jax.numpy as jnp
from jax import lax
from jax.experimental import pallas as pl
from jax.experimental.pallas import tpu as pltpu
from jax.sharding import PartitionSpec as P

HEADS = 6
DH = 128
C = 768
KW = 5
POOL = 16
ROWS = 512
TOK = 32
SEG_TOK = 512
CTX = 16
NZ = 8
PLANE = 32
BLK = 48
PARTS = 3
SUB = 16
CHIPS = 16
XW = 256
EPSILON = 1e-06
GELU_SCALE = 0.7978845608028654
CUBIC = 0.044715
MESH = pl.DeviceIdType.MESH
F32 = jnp.float32
BF16 = jnp.bfloat16


def dot(a, b):
    return jnp.dot(a, b, preferred_element_type=F32)


def dot_rt(a, b):
    return lax.dot_general(a, b, (((1,), (1,)), ((), ())), preferred_element_type=F32)


def window_matrix(first, columns):
    row = lax.broadcasted_iota(jnp.int32, (KW * TOK, columns), 0)
    low = (row % TOK) * POOL + row // TOK - 2
    place = lax.broadcasted_iota(jnp.int32, (KW * TOK, columns), 1) + first
    return jnp.where((place >= low) & (place < low + POOL), 1.0, 0.0).astype(BF16)


def body(
    feat_h, base_h, table_h, gain_h, wc_h, wq_h, wk_h, wv_h, wo_h, cot_h,
    grad_in_ref, grad_conv_ref,
    feat, base, table, gain, wc, wq, wk, wv, wo, cot,
    emb, act, normed, inv, slope, win, halo, xs, xr, xt,
    qs, hb, pt, gst, go, gb, perm, grp, grr, grh, grs, rs, rr, edge,
    in_sem, send_sem, recv_sem,
):
    dp = lax.axis_index("dp")
    ctx = lax.axis_index("ctx")
    zz = dp // 2
    hi = dp % 2
    me = hi * CTX + ctx
    core = ctx % 2
    chip = me // 2
    slot = core * CHIPS + chip

    def plane_id(p):
        return {"dp": zz * 2 + p // CTX, "ctx": p % CTX}

    def z_id(z):
        return {"dp": z * 2 + hi, "ctx": ctx}

    pairs = [
        (base_h, base), (table_h, table), (gain_h, gain), (feat_h, feat), (cot_h, cot), (wo_h, wo),
        (wc_h, wc), (wq_h, wq), (wk_h, wk), (wv_h, wv),
    ]
    loads = [pltpu.make_async_copy(s, d, in_sem.at[i]) for i, (s, d) in enumerate(pairs)]
    for load in loads:
        load.start()

    barrier = pltpu.get_barrier_semaphore()

    @pl.loop(1, PLANE)
    def _(i):
        pl.semaphore_signal(barrier, inc=1, device_id=plane_id((me + i) % PLANE), device_id_type=MESH)

    @pl.loop(1, NZ)
    def _(i):
        pl.semaphore_signal(barrier, inc=1, device_id=z_id((zz + i) % NZ), device_id_type=MESH)

    win[...] = window_matrix(0, ROWS)
    col = lax.broadcasted_iota(jnp.int32, (C, C), 1)
    group = col // 128
    channel = (2 * (col % 128 // SUB) + group % 2) * BLK + group // 2 * SUB + col % SUB
    perm[...] = jnp.where(channel == lax.broadcasted_iota(jnp.int32, (C, C), 0), 1.0, 0.0).astype(BF16)
    for load in loads[:4]:
        load.wait()

    base_col = jnp.broadcast_to(base[...], (128, ROWS)).T
    onehot = jnp.where(
        base_col == lax.broadcasted_iota(jnp.int32, (ROWS, 128), 1), 1.0, 0.0
    ).astype(BF16)
    row_id = lax.broadcasted_iota(jnp.int32, (128, C), 0)
    tab = jnp.zeros((128, C), F32)
    for b in range(4):
        tab = jnp.where(row_id == b, table[b : b + 1, :].astype(F32), tab)
    tab = tab.astype(BF16)
    emb[...] = dot(onehot, tab).astype(BF16)
    gain_f = gain[...].astype(F32)[None]

    def rows_forward(r0):
        rows = pl.ds(r0, POOL)
        s = feat[rows, :].astype(F32) + emb[rows, :].astype(F32)
        scale = lax.rsqrt(jnp.mean(s * s, axis=-1, keepdims=True) + EPSILON)
        n = s * scale
        u = n * gain_f
        t = jnp.tanh(GELU_SCALE * (u + CUBIC * (u * u * u)))
        act[rows, :] = (0.5 * u * (1.0 + t)).astype(BF16)
        normed[rows, :] = n
        inv[rows, :] = scale

    rows_forward(0)
    rows_forward(ROWS - POOL)
    @pl.loop(1, ROWS // POOL // 2)
    def _(i):
        rows_forward(pl.multiple_of(i * POOL, POOL))

    pl.semaphore_wait(barrier, PLANE - 1 + NZ - 1)

    def sides(first, last, into, sem):
        low = pltpu.make_async_remote_copy(
            src_ref=first, dst_ref=into.at[1], send_sem=send_sem.at[sem], recv_sem=recv_sem.at[sem],
            device_id={"dp": dp, "ctx": jnp.maximum(ctx - 1, 0)}, device_id_type=MESH,
        )
        high = pltpu.make_async_remote_copy(
            src_ref=last, dst_ref=into.at[0], send_sem=send_sem.at[sem + 1], recv_sem=recv_sem.at[sem + 1],
            device_id={"dp": dp, "ctx": jnp.minimum(ctx + 1, CTX - 1)}, device_id_type=MESH,
        )

        @pl.when(ctx > 0)
        def _():
            low.start()

        @pl.when(ctx < CTX - 1)
        def _():
            high.start()

        @pl.when(ctx == 0)
        def _():
            into[0] = jnp.zeros((16, C), BF16)

        @pl.when(ctx == CTX - 1)
        def _():
            into[1] = jnp.zeros((16, C), BF16)

        return low, high

    def sides_arrive(copies):
        low, high = copies

        @pl.when(ctx < CTX - 1)
        def _():
            low.wait_recv()

        @pl.when(ctx > 0)
        def _():
            high.wait_recv()

    def sides_sent(copies):
        low, high = copies

        @pl.when(ctx > 0)
        def _():
            low.wait_send()

        @pl.when(ctx < CTX - 1)
        def _():
            high.wait_send()

    act_sides = sides(act.at[pl.ds(0, 16), :], act.at[pl.ds(ROWS - 16, 16), :], halo, 0)

    @pl.loop(ROWS // POOL // 2, ROWS // POOL - 1)
    def _(i):
        rows_forward(pl.multiple_of(i * POOL, POOL))

    sums = dot(win[...], act[...])
    mean_rows = win[2 * TOK : 3 * TOK, :]
    counts = dot(mean_rows, onehot).astype(BF16)
    pooled_in = dot(mean_rows, feat[...]) + dot(counts, tab)

    loads[4].wait()
    loads[5].wait()
    grad_attn = dot_rt(cot[...], wo[...]).astype(BF16)
    for h in range(HEADS):
        qs[h, 3] = grad_attn[:, h * DH : (h + 1) * DH]

    sides_arrive(act_sides)
    edge_win = jnp.concatenate([window_matrix(-16, 16), window_matrix(ROWS, 16)], axis=1)
    sums = sums + dot(edge_win, jnp.concatenate([halo[0], halo[1]], axis=0))
    high_part = sums.astype(BF16)
    low_part = (sums - high_part.astype(F32)).astype(BF16)

    for c in range(CTX):
        cols = [sums[j * TOK : (j + 1) * TOK, c * BLK : (c + 1) * BLK] for j in range(KW)]
        cols.append(jnp.zeros((TOK, XW - KW * BLK), F32))
        xs[c] = jnp.concatenate(cols, axis=1).astype(BF16)

    other = 1 - hi

    def x_send(half, c):
        return pltpu.make_async_remote_copy(
            src_ref=xs.at[c], dst_ref=xr.at[slot], send_sem=send_sem.at[10], recv_sem=recv_sem.at[5],
            device_id={"dp": zz * 2 + half, "ctx": c}, device_id_type=MESH,
        )

    @pl.loop(1, CTX)
    def _(i):
        x_send(hi, (ctx + i) % CTX).start()

    loads[6].wait()
    conv = jnp.zeros((2 * TOK, C), F32)
    for j in range(KW):
        part = slice(j * TOK, (j + 1) * TOK)
        conv = conv + dot(jnp.concatenate([high_part[part], low_part[part]], axis=0), wc[j])
    pooled = ((pooled_in + conv[:TOK] + conv[TOK:]) * (1.0 / POOL)).astype(BF16)

    for i in range(7, 10):
        loads[i].wait()
    for k, weight in enumerate((wq, wk, wv)):
        made = dot(pooled, weight[...]).astype(BF16)
        for h in range(HEADS):
            qs[h, k] = made[:, h * DH : (h + 1) * DH]

    def to_head(h):
        return pltpu.make_async_remote_copy(
            src_ref=qs.at[h], dst_ref=hb.at[:, pl.ds(pl.multiple_of(ctx * TOK, TOK), TOK), :],
            send_sem=send_sem.at[4 + h], recv_sem=recv_sem.at[4],
            device_id={"dp": dp, "ctx": 2 * h}, device_id_type=MESH,
        )

    for h in range(HEADS):
        @pl.when(ctx != 2 * h)
        def _():
            to_head(h).start()

    @pl.loop(0, CTX)
    def _(i):
        x_send(other, (ctx + i) % CTX).start()

    xr[slot] = xs[ctx]

    head = ctx // 2
    is_head = (ctx % 2 == 0) & (ctx < 2 * HEADS)

    def from_head(c):
        return pltpu.make_async_remote_copy(
            src_ref=go.at[c], dst_ref=gb.at[head],
            send_sem=send_sem.at[11], recv_sem=recv_sem.at[6],
            device_id={"dp": dp, "ctx": c}, device_id_type=MESH,
        )

    @pl.when(is_head)
    def _():
        hb[:, pl.ds(pl.multiple_of(ctx * TOK, TOK), TOK), :] = qs[head]
        arrived = hb.at[:, pl.ds(0, SEG_TOK - TOK), :]
        pltpu.make_async_copy(arrived, arrived, recv_sem.at[4]).wait()
        scale = 1.0 / DH**0.5
        keys = hb[1]
        values = hb[2]
        values_t = values.T

        @pl.loop(0, SEG_TOK // 128)
        def _(i):
            part = pl.ds(pl.multiple_of(i * 128, 128), 128)
            query = hb[0, part, :]
            grad = hb[3, part, :]
            score = dot_rt(keys, query) * scale
            expo = jnp.exp(score - jnp.max(score, axis=0, keepdims=True))
            prob = expo * (1.0 / jnp.sum(expo, axis=0, keepdims=True))
            prob_b = prob.astype(BF16)
            out_t = dot(values_t, prob_b).astype(BF16).astype(F32)
            delta = jnp.sum(grad.T.astype(F32) * out_t, axis=0, keepdims=True)
            grad_prob = dot_rt(values, grad)
            pt[:, part] = prob_b
            gst[:, part] = (prob * (grad_prob - delta) * scale).astype(BF16)

        go[:, 0] = dot(keys.T, gst[...]).T.astype(BF16).reshape(CTX, TOK, DH)
        go[:, 1] = dot(gst[...], hb[0]).astype(BF16).reshape(CTX, TOK, DH)
        go[:, 2] = dot(pt[...], hb[3]).astype(BF16).reshape(CTX, TOK, DH)

        @pl.loop(1, CTX)
        def _(i):
            from_head((ctx + i) % CTX).start()

        gb[head] = go[ctx]
        five = gb.at[pl.ds(0, HEADS - 1)]
        pltpu.make_async_copy(five, five, recv_sem.at[6]).wait()

    @pl.when(jnp.logical_not(is_head))
    def _():
        pltpu.make_async_copy(gb, gb, recv_sem.at[6]).wait()

    grad_pooled = cot[...].astype(F32)
    for k, weight in enumerate((wq, wk, wv)):
        whole = jnp.concatenate([gb[h, k] for h in range(HEADS)], axis=1)
        grad_pooled = grad_pooled + dot_rt(whole, weight[...])
    grs[...] = (grad_pooled * (1.0 / POOL)).astype(BF16)
    sorted_g = dot(grs[...], perm[...]).astype(BF16)
    for k in range(PARTS):
        for h in range(2):
            first = (2 * k + h) * 128
            grp[k, h] = sorted_g[:, first : first + 128]

    for k in range(PARTS):
        @pl.loop(1, CHIPS)
        def _(i):
            to = (chip + i) % CHIPS
            pltpu.make_async_remote_copy(
                src_ref=grp.at[k, to // (CHIPS // 2)], dst_ref=grr.at[k, slot],
                send_sem=send_sem.at[12], recv_sem=recv_sem.at[7 + k],
                device_id=plane_id(2 * to + core), device_id_type=MESH,
            ).start()

        grr[k, slot] = grp[k, hi]

    row_sides = sides(grs.at[pl.ds(0, 16), :], grs.at[pl.ds(16, 16), :], grh, 2)

    @pl.loop(0, ROWS // POOL)
    def _(i):
        rows = pl.ds(pl.multiple_of(i * POOL, POOL), POOL)
        u = normed[rows, :] * gain_f
        square = u * u
        t = jnp.tanh(GELU_SCALE * (u + CUBIC * (square * u)))
        d = 0.5 * (1.0 + t) + 0.5 * u * (1.0 - t * t) * GELU_SCALE * (1.0 + 3.0 * CUBIC * square)
        slope[rows, :] = d * gain_f

    others = xr.at[pl.ds(0, PLANE - 1)]
    pltpu.make_async_copy(others, others, recv_sem.at[5]).wait()
    for i in range(PLANE * TOK // 128):
        block = xr[4 * i : 4 * i + 4].reshape(128, XW)
        xt[:, i * 128 : (i + 1) * 128] = block.T

    factor = 1.0 / (CTX * CTX * ROWS) ** 0.5

    def pass_on(k):
        mine = grr.at[k, pl.ds(pl.multiple_of(core * CHIPS, CHIPS), CHIPS)]
        return pltpu.make_async_remote_copy(
            src_ref=mine, dst_ref=mine, send_sem=send_sem.at[14 + k], recv_sem=recv_sem.at[11 + k],
            device_id={"dp": dp, "ctx": ctx + 1 - 2 * core}, device_id_type=MESH,
        )

    def forward(k):
        others = grr.at[k, pl.ds(0, CHIPS - 1)]
        pltpu.make_async_copy(others, others, recv_sem.at[7 + k]).wait()
        pass_on(k).start()

    def multiply(k):
        pass_on(k).wait_recv()
        made = dot(xt[...], grr[k].reshape(PLANE * TOK, 128)) * factor
        rs[k] = made.T.astype(BF16)

        @pl.loop(1, NZ)
        def _(i):
            z = (zz + i) % NZ
            pltpu.make_async_remote_copy(
                src_ref=rs.at[k, pl.ds(pl.multiple_of(z * SUB, SUB), SUB), :], dst_ref=rr.at[zz, k],
                send_sem=send_sem.at[13], recv_sem=recv_sem.at[10],
                device_id=z_id(z), device_id_type=MESH,
            ).start()

        rr[zz, k] = rs[k, pl.ds(pl.multiple_of(zz * SUB, SUB), SUB), :]

    forward(0)
    forward(1)
    multiply(0)
    forward(2)
    multiply(1)
    multiply(2)

    sides_arrive(row_sides)
    ext = jnp.concatenate([grh[0], grs[...], grh[1]], axis=0)
    first0 = first1 = mid = last0 = last1 = None
    for j in range(KW):
        y = dot_rt(ext, wc[j])
        own, before, after = y[16:48], y[15:47], y[17:49]
        terms = (
            before if j >= 3 else own,
            before if j >= 4 else own,
            own,
            after if j < 1 else own,
            after if j < 2 else own,
        )
        if j == 0:
            first0, first1, mid, last0, last1 = terms
        else:
            first0, first1, mid, last0, last1 = (
                a + b for a, b in zip((first0, first1, mid, last0, last1), terms)
            )
    for k, value in enumerate((first0, first1, mid, last0, last1, grs[...].astype(F32))):
        edge[k] = value

    in_group = lax.broadcasted_iota(jnp.int32, (POOL, C), 0)

    @pl.loop(0, TOK)
    def _(i):
        rows = pl.ds(pl.multiple_of(i * POOL, POOL), POOL)
        one = pl.ds(i, 1)
        g = jnp.broadcast_to(edge[2, one, :], (POOL, C))
        for r, k in ((0, 0), (1, 1), (14, 3), (15, 4)):
            g = jnp.where(in_group == r, edge[k, one, :], g)
        g = g * slope[rows, :]
        n = normed[rows, :]
        mean = jnp.mean(g * n, axis=-1, keepdims=True)
        grad_in_ref[rows, :] = (edge[5, one, :] + inv[rows, :] * (g - n * mean)).astype(BF16)

    others = rr.at[pl.ds(0, NZ - 1)]
    pltpu.make_async_copy(others, others, recv_sem.at[10]).wait()
    total = rr[0].astype(F32)
    for z in range(1, NZ):
        total = total + rr[z].astype(F32)
    grad_conv_ref[...] = total.reshape(BLK, XW)

    sides_sent(act_sides)
    sides_sent(row_sides)
    for h in range(HEADS):
        @pl.when(ctx != 2 * h)
        def _():
            to_head(h).wait_send()
    part = xr.at[pl.ds(0, PLANE - 1)]
    pltpu.make_async_copy(part, part, send_sem.at[10]).wait()

    @pl.when(is_head)
    def _():
        part = go.at[pl.ds(0, CTX - 1)]
        pltpu.make_async_copy(part, part, send_sem.at[11]).wait()

    part = grr.at[:, pl.ds(0, CHIPS - 1)]
    pltpu.make_async_copy(part, part, send_sem.at[12]).wait()
    for k in range(PARTS):
        pass_on(k).wait_send()
    part = rr.at[pl.ds(0, NZ - 1)]
    pltpu.make_async_copy(part, part, send_sem.at[13]).wait()


def per_device(
    features, bases, dna_table, norm_gain, w_conv, w_query, w_key, w_value, w_out, cotangent
):
    vmem = pltpu.VMEM
    scratch = [
        vmem((ROWS, C), BF16), vmem((1, ROWS), jnp.int32), vmem((4, C), BF16), vmem((C,), BF16),
        vmem((KW, C, C), BF16), vmem((C, C), BF16), vmem((C, C), BF16), vmem((C, C), BF16),
        vmem((C, C), BF16), vmem((TOK, C), BF16),
        vmem((ROWS, C), BF16),
        vmem((ROWS, C), BF16),
        vmem((ROWS, C), F32),
        vmem((ROWS, 1), F32),
        vmem((ROWS, C), F32),
        vmem((KW * TOK, ROWS), BF16),
        vmem((2, 16, C), BF16),
        vmem((CTX, TOK, XW), BF16),
        vmem((PLANE, TOK, XW), BF16),
        vmem((XW, PLANE * TOK), BF16),
        vmem((HEADS, 4, TOK, DH), BF16),
        vmem((4, SEG_TOK, DH), BF16),
        vmem((SEG_TOK, SEG_TOK), BF16),
        vmem((SEG_TOK, SEG_TOK), BF16),
        vmem((CTX, 3, TOK, DH), BF16),
        vmem((HEADS, 3, TOK, DH), BF16),
        vmem((C, C), BF16),
        vmem((PARTS, 2, TOK, 128), BF16),
        vmem((PARTS, PLANE, TOK, 128), BF16),
        vmem((2, 16, C), BF16),
        vmem((TOK, C), BF16),
        vmem((PARTS, 128, XW), BF16),
        vmem((NZ, PARTS, SUB, XW), BF16),
        vmem((6, TOK, C), F32),
        pltpu.SemaphoreType.DMA((10,)),
        pltpu.SemaphoreType.DMA((17,)),
        pltpu.SemaphoreType.DMA((14,)),
    ]
    grad_in, grad_conv = pl.pallas_call(
        body,
        out_shape=(
            jax.ShapeDtypeStruct((ROWS, C), BF16),
            jax.ShapeDtypeStruct((BLK, XW), F32),
        ),
        in_specs=[pl.BlockSpec(memory_space=pltpu.HBM)] * 10,
        out_specs=(pl.BlockSpec(memory_space=pltpu.VMEM),) * 2,
        scratch_shapes=scratch,
        compiler_params=pltpu.CompilerParams(
            collective_id=0, has_side_effects=True, vmem_limit_bytes=56 * 1024 * 1024
        ),
        cost_estimate=pl.CostEstimate(flops=10**9, bytes_accessed=12 * 10**6, transcendentals=10**6),
    )(
        features[0], bases, dna_table, norm_gain, w_conv, w_query, w_key, w_value, w_out,
        cotangent[0],
    )
    grad_conv = grad_conv[:, : KW * BLK].reshape(BLK, KW, BLK).transpose(2, 1, 0)
    return grad_in[None], grad_conv


def solution(mesh):
    in_specs = (
        P("dp", "ctx", None),
        P("dp", "ctx"),
        P(),
        P(),
        P(),
        P(),
        P(),
        P(),
        P(),
        P("dp", "ctx", None),
    )
    out_specs = (P("dp", "ctx", None), P("ctx", None, "dp"))
    return jax.shard_map(
        per_device, mesh=mesh, in_specs=in_specs, out_specs=out_specs, check_vma=False
    )
```

```python
import functools

import jax
import jax.numpy as jnp
from jax import lax
from jax.experimental import pallas as pl
from jax.experimental.pallas import tpu as pltpu
from jax.sharding import PartitionSpec as P

HEADS = 6
DH = 128
C = 768
KW = 5
POOL = 16
ROWS = 512
TOK = 32
SEG_TOK = 512
CTX = 16
NZ = 8
PLANE = 32
BLK = 48
PARTS = 3
SUB = 16
COPIES = 4
CHIPS = 16
XW = 256
EPSILON = 1e-06
GELU_SCALE = 0.7978845608028654
CUBIC = 0.044715
MESH = pl.DeviceIdType.MESH
F32 = jnp.float32
BF16 = jnp.bfloat16


PLACE = (0, 2, 4, 8, 12, 14)


def dot(a, b):
    return jnp.dot(a, b, preferred_element_type=F32)


def dot_rt(a, b):
    return lax.dot_general(a, b, (((1,), (1,)), ((), ())), preferred_element_type=F32)


def window_matrix(first, columns):
    row = lax.broadcasted_iota(jnp.int32, (KW * TOK, columns), 0)
    low = (row % TOK) * POOL + row // TOK - 2
    place = lax.broadcasted_iota(jnp.int32, (KW * TOK, columns), 1) + first
    return jnp.where((place >= low) & (place < low + POOL), 1.0, 0.0).astype(BF16)


def body(
    feat_h, base_h, table_h, gain_h, wc_h, wq_h, wk_h, wv_h, wo_h, cot_h,
    grad_in_h, grad_conv_ref,
    feat, base, table, gain, wc, wq, wk, wv, wo, cot,
    emb, act, normed, inv, slope, win, halo, xs, xr, xt,
    qs, hb, pt, gst, go, gb, perm, grp, grr, grh, grs, rs, rr, edge, grad_in_ref,
    in_sem, send_sem, recv_sem,
):
    dp = lax.axis_index("dp")
    ctx = lax.axis_index("ctx")
    zz = dp // 2
    hi = dp % 2
    me = hi * CTX + ctx
    core = ctx % 2
    chip = me // 2
    slot = core * CHIPS + chip
    pair = ctx // 2
    head = pair - pair // 4 - pair // 6
    is_head = (core == 0) & (pair != 3) & (pair != 5)

    def plane_id(p):
        return {"dp": zz * 2 + p // CTX, "ctx": p % CTX}

    def z_id(z):
        return {"dp": z * 2 + hi, "ctx": ctx}

    pairs = [
        (base_h, base), (table_h, table), (gain_h, gain), (feat_h, feat), (cot_h, cot), (wo_h, wo),
        (wc_h, wc), (wq_h, wq), (wk_h, wk), (wv_h, wv),
    ]
    loads = [pltpu.make_async_copy(s, d, in_sem.at[i]) for i, (s, d) in enumerate(pairs)]
    for load in loads:
        load.start()

    barrier = pltpu.get_barrier_semaphore()

    @pl.loop(1, PLANE)
    def _(i):
        pl.semaphore_signal(barrier, inc=1, device_id=plane_id((me + i) % PLANE), device_id_type=MESH)

    @pl.loop(1, NZ)
    def _(i):
        pl.semaphore_signal(barrier, inc=1, device_id=z_id((zz + i) % NZ), device_id_type=MESH)

    win[...] = window_matrix(0, ROWS)
    col = lax.broadcasted_iota(jnp.int32, (C, C), 1)
    group = col // 128
    channel = (2 * (col % 128 // SUB) + group % 2) * BLK + group // 2 * SUB + col % SUB
    perm[...] = jnp.where(channel == lax.broadcasted_iota(jnp.int32, (C, C), 0), 1.0, 0.0).astype(BF16)
    for load in loads[:4]:
        load.wait()

    base_col = jnp.broadcast_to(base[...], (128, ROWS)).T
    onehot = jnp.where(
        base_col == lax.broadcasted_iota(jnp.int32, (ROWS, 128), 1), 1.0, 0.0
    ).astype(BF16)
    row_id = lax.broadcasted_iota(jnp.int32, (128, C), 0)
    tab = jnp.zeros((128, C), F32)
    for b in range(4):
        tab = jnp.where(row_id == b, table[b : b + 1, :].astype(F32), tab)
    tab = tab.astype(BF16)
    emb[...] = dot(onehot, tab).astype(BF16)
    gain_f = gain[...].astype(F32)[None]

    def rows_forward(r0):
        rows = pl.ds(r0, POOL)
        s = feat[rows, :].astype(F32) + emb[rows, :].astype(F32)
        scale = lax.rsqrt(jnp.mean(s * s, axis=-1, keepdims=True) + EPSILON)
        n = s * scale
        u = n * gain_f
        t = jnp.tanh(GELU_SCALE * (u + CUBIC * (u * u * u)))
        act[rows, :] = (0.5 * u * (1.0 + t)).astype(BF16)
        normed[rows, :] = n
        inv[rows, :] = scale

    rows_forward(0)
    rows_forward(ROWS - POOL)
    @pl.loop(1, ROWS // POOL // 2, unroll=3)
    def _(i):
        rows_forward(pl.multiple_of(i * POOL, POOL))

    pl.semaphore_wait(barrier, PLANE - 1 + NZ - 1)

    def sides(first, last, into, sem):
        low = pltpu.make_async_remote_copy(
            src_ref=first, dst_ref=into.at[1], send_sem=send_sem.at[sem], recv_sem=recv_sem.at[sem],
            device_id={"dp": dp, "ctx": jnp.maximum(ctx - 1, 0)}, device_id_type=MESH,
        )
        high = pltpu.make_async_remote_copy(
            src_ref=last, dst_ref=into.at[0], send_sem=send_sem.at[sem + 1], recv_sem=recv_sem.at[sem + 1],
            device_id={"dp": dp, "ctx": jnp.minimum(ctx + 1, CTX - 1)}, device_id_type=MESH,
        )

        @pl.when(ctx > 0)
        def _():
            low.start()

        @pl.when(ctx < CTX - 1)
        def _():
            high.start()

        @pl.when(ctx == 0)
        def _():
            into[0] = jnp.zeros((16, C), BF16)

        @pl.when(ctx == CTX - 1)
        def _():
            into[1] = jnp.zeros((16, C), BF16)

        return low, high

    def sides_arrive(copies):
        low, high = copies

        @pl.when(ctx < CTX - 1)
        def _():
            low.wait_recv()

        @pl.when(ctx > 0)
        def _():
            high.wait_recv()

    def sides_sent(copies):
        low, high = copies

        @pl.when(ctx > 0)
        def _():
            low.wait_send()

        @pl.when(ctx < CTX - 1)
        def _():
            high.wait_send()

    act_sides = sides(act.at[pl.ds(0, 16), :], act.at[pl.ds(ROWS - 16, 16), :], halo, 0)

    @pl.loop(ROWS // POOL // 2, ROWS // POOL - 1, unroll=3)
    def _(i):
        rows_forward(pl.multiple_of(i * POOL, POOL))

    sums = dot(win[...], act[...])
    mean_rows = win[2 * TOK : 3 * TOK, :]
    counts = dot(mean_rows, onehot).astype(BF16)
    pooled_in = dot(mean_rows, feat[...]) + dot(counts, tab)

    loads[4].wait()
    loads[5].wait()
    grad_attn = dot_rt(cot[...], wo[...]).astype(BF16)
    for h in range(HEADS):
        qs[h, 3] = grad_attn[:, h * DH : (h + 1) * DH]

    def to_head(h, k):
        return pltpu.make_async_remote_copy(
            src_ref=qs.at[h, k], dst_ref=hb.at[k, pl.ds(pl.multiple_of(ctx * TOK, TOK), TOK), :],
            send_sem=send_sem.at[4 + k], recv_sem=recv_sem.at[14 + k],
            device_id={"dp": dp, "ctx": PLACE[h]}, device_id_type=MESH,
        )

    def to_heads(k):
        for h in range(HEADS):
            @pl.when(ctx != PLACE[h])
            def _():
                to_head(h, k).start()

    to_heads(3)

    sides_arrive(act_sides)
    edge_win = jnp.concatenate([window_matrix(-16, 16), window_matrix(ROWS, 16)], axis=1)
    sums = sums + dot(edge_win, jnp.concatenate([halo[0], halo[1]], axis=0))
    high_part = sums.astype(BF16)
    low_part = (sums - high_part.astype(F32)).astype(BF16)

    for c in range(CTX):
        cols = [sums[j * TOK : (j + 1) * TOK, c * BLK : (c + 1) * BLK] for j in range(KW)]
        cols.append(jnp.zeros((TOK, XW - KW * BLK), F32))
        xs[c] = jnp.concatenate(cols, axis=1).astype(BF16)

    other = 1 - hi

    def x_send(half, c):
        return pltpu.make_async_remote_copy(
            src_ref=xs.at[c], dst_ref=xr.at[slot], send_sem=send_sem.at[10], recv_sem=recv_sem.at[5],
            device_id={"dp": zz * 2 + half, "ctx": c}, device_id_type=MESH,
        )

    @pl.loop(1, CTX)
    def _(i):
        x_send(hi, (ctx + i) % CTX).start()

    loads[6].wait()
    conv = jnp.zeros((2 * TOK, C), F32)
    for j in range(KW):
        part = slice(j * TOK, (j + 1) * TOK)
        conv = conv + dot(jnp.concatenate([high_part[part], low_part[part]], axis=0), wc[j])
    pooled = ((pooled_in + conv[:TOK] + conv[TOK:]) * (1.0 / POOL)).astype(BF16)

    for i in range(7, 10):
        loads[i].wait()
    for k, weight in ((1, wk), (0, wq), (2, wv)):
        made = dot(pooled, weight[...]).astype(BF16)
        for h in range(HEADS):
            qs[h, k] = made[:, h * DH : (h + 1) * DH]
        to_heads(k)

    @pl.loop(0, CTX)
    def _(i):
        x_send(other, (ctx + i) % CTX).start()

    xr[slot] = xs[ctx]

    def from_head(c, k):
        return pltpu.make_async_remote_copy(
            src_ref=go.at[c, k], dst_ref=gb.at[head, k],
            send_sem=send_sem.at[11], recv_sem=recv_sem.at[6],
            device_id={"dp": dp, "ctx": c}, device_id_type=MESH,
        )

    def from_heads(k):
        @pl.loop(1, CTX)
        def _(i):
            from_head((ctx + i) % CTX, k).start()

    @pl.when(is_head)
    def _():
        hb[:, pl.ds(pl.multiple_of(ctx * TOK, TOK), TOK), :] = qs[head]
        for k in range(4):
            arrived = hb.at[k, pl.ds(0, SEG_TOK - TOK), :]
            pltpu.make_async_copy(arrived, arrived, recv_sem.at[14 + k]).wait()
        scale = 1.0 / DH**0.5
        keys = hb[1]
        values = hb[2]
        values_t = values.T
        keys_t = keys.T

        @pl.loop(0, SEG_TOK // 128)
        def _(i):
            part = pl.ds(pl.multiple_of(i * 128, 128), 128)
            query = hb[0, part, :]
            grad = hb[3, part, :]
            score = dot_rt(keys, query) * scale
            expo = jnp.exp(score - jnp.max(score, axis=0, keepdims=True))
            prob = expo * (1.0 / jnp.sum(expo, axis=0, keepdims=True))
            prob_b = prob.astype(BF16)
            out_t = dot(values_t, prob_b).astype(BF16).astype(F32)
            delta = jnp.sum(grad.T.astype(F32) * out_t, axis=0, keepdims=True)
            grad_prob = dot_rt(values, grad)
            pt[:, part] = prob_b
            grad_score = (prob * (grad_prob - delta) * scale).astype(BF16)
            gst[:, part] = grad_score
            grad_query = dot(keys_t, grad_score).T.astype(BF16).reshape(4, TOK, DH)
            for m in range(4):
                go[4 * i + m, 0] = grad_query[m]
                @pl.when(ctx != 4 * i + m)
                def _():
                    from_head(4 * i + m, 0).start()

        go[:, 2] = dot(pt[...], hb[3]).astype(BF16).reshape(CTX, TOK, DH)
        from_heads(2)
        go[:, 1] = dot(gst[...], hb[0]).astype(BF16).reshape(CTX, TOK, DH)
        from_heads(1)
        gb[head] = go[ctx]
        five = gb.at[pl.ds(0, HEADS - 1)]
        pltpu.make_async_copy(five, five, recv_sem.at[6]).wait()

    @pl.when(jnp.logical_not(is_head))
    def _():
        pltpu.make_async_copy(gb, gb, recv_sem.at[6]).wait()

    grad_pooled = cot[...].astype(F32)
    for k, weight in enumerate((wq, wk, wv)):
        whole = jnp.concatenate([gb[h, k] for h in range(HEADS)], axis=1)
        grad_pooled = grad_pooled + dot_rt(whole, weight[...])
    grs[...] = (grad_pooled * (1.0 / POOL)).astype(BF16)
    sorted_g = dot(grs[...], perm[...]).astype(BF16)
    for k in range(PARTS):
        for h in range(2):
            first = (2 * k + h) * 128
            grp[k, h] = sorted_g[:, first : first + 128]

    for k in range(PARTS):
        @pl.loop(1, CHIPS)
        def _(i):
            to = (chip + i) % CHIPS
            pltpu.make_async_remote_copy(
                src_ref=grp.at[k, to // (CHIPS // 2)], dst_ref=grr.at[k, slot],
                send_sem=send_sem.at[12], recv_sem=recv_sem.at[7 + k],
                device_id=plane_id(2 * to + core), device_id_type=MESH,
            ).start()

        grr[k, slot] = grp[k, hi]

    row_sides = sides(grs.at[pl.ds(0, 16), :], grs.at[pl.ds(16, 16), :], grh, 2)

    @pl.loop(0, ROWS // POOL, unroll=2)
    def _(i):
        rows = pl.ds(pl.multiple_of(i * POOL, POOL), POOL)
        u = normed[rows, :] * gain_f
        square = u * u
        t = jnp.tanh(GELU_SCALE * (u + CUBIC * (square * u)))
        d = 0.5 * (1.0 + t) + 0.5 * u * (1.0 - t * t) * GELU_SCALE * (1.0 + 3.0 * CUBIC * square)
        slope[rows, :] = d * gain_f

    others = xr.at[pl.ds(0, PLANE - 1)]
    pltpu.make_async_copy(others, others, recv_sem.at[5]).wait()
    for i in range(PLANE * TOK // 128):
        block = xr[4 * i : 4 * i + 4].reshape(128, XW)
        xt[:, i * 128 : (i + 1) * 128] = block.T

    factor = 1.0 / (CTX * CTX * ROWS) ** 0.5

    def pass_on(k):
        mine = grr.at[k, pl.ds(pl.multiple_of(core * CHIPS, CHIPS), CHIPS)]
        return pltpu.make_async_remote_copy(
            src_ref=mine, dst_ref=mine, send_sem=send_sem.at[14 + k], recv_sem=recv_sem.at[11 + k],
            device_id={"dp": dp, "ctx": ctx + 1 - 2 * core}, device_id_type=MESH,
        )

    def forward(k):
        others = grr.at[k, pl.ds(0, CHIPS - 1)]
        pltpu.make_async_copy(others, others, recv_sem.at[7 + k]).wait()
        pass_on(k).start()

    def multiply(k):
        pass_on(k).wait_recv()
        made = dot(xt[...], grr[k].reshape(PLANE * TOK, 128)) * factor
        rs[k] = made.T.astype(BF16)

        @pl.loop(1, NZ)
        def _(i):
            z = (zz + i) % NZ
            pltpu.make_async_remote_copy(
                src_ref=rs.at[k, pl.ds(pl.multiple_of(z * SUB, SUB), SUB), :], dst_ref=rr.at[zz, k],
                send_sem=send_sem.at[13], recv_sem=recv_sem.at[10],
                device_id=z_id(z), device_id_type=MESH,
            ).start()

        rr[zz, k] = rs[k, pl.ds(pl.multiple_of(zz * SUB, SUB), SUB), :]

    forward(0)
    forward(1)
    multiply(0)
    forward(2)
    multiply(1)
    multiply(2)

    sides_arrive(row_sides)
    ext = jnp.concatenate([grh[0], grs[...], grh[1]], axis=0)
    first0 = first1 = mid = last0 = last1 = None
    for j in range(KW):
        y = dot_rt(ext, wc[j])
        own, before, after = y[16:48], y[15:47], y[17:49]
        terms = (
            before if j >= 3 else own,
            before if j >= 4 else own,
            own,
            after if j < 1 else own,
            after if j < 2 else own,
        )
        if j == 0:
            first0, first1, mid, last0, last1 = terms
        else:
            first0, first1, mid, last0, last1 = (
                a + b for a, b in zip((first0, first1, mid, last0, last1), terms)
            )
    for k, value in enumerate((first0, first1, mid, last0, last1, grs[...].astype(F32))):
        edge[k] = value

    in_group = lax.broadcasted_iota(jnp.int32, (POOL, C), 0)

    @pl.loop(0, TOK, unroll=2)
    def _(i):
        rows = pl.ds(pl.multiple_of(i * POOL, POOL), POOL)
        one = pl.ds(i, 1)
        g = jnp.broadcast_to(edge[2, one, :], (POOL, C))
        for r, k in ((0, 0), (1, 1), (14, 3), (15, 4)):
            g = jnp.where(in_group == r, edge[k, one, :], g)
        g = g * slope[rows, :]
        n = normed[rows, :]
        mean = jnp.mean(g * n, axis=-1, keepdims=True)
        grad_in_ref[rows, :] = (edge[5, one, :] + inv[rows, :] * (g - n * mean)).astype(BF16)

    grad_in_out = pltpu.make_async_copy(grad_in_ref, grad_in_h, in_sem.at[10])
    grad_in_out.start()

    others = rr.at[pl.ds(0, NZ - 1)]
    pltpu.make_async_copy(others, others, recv_sem.at[10]).wait()
    total = rr[0].astype(F32)
    for z in range(1, NZ):
        total = total + rr[z].astype(F32)
    total = jnp.concatenate([total.reshape(BLK, XW), jnp.zeros((128 - BLK, XW), F32)], axis=0).T
    for j in range(KW):
        grad_conv_ref[j] = total[j * BLK : (j + 1) * BLK, :BLK]

    grad_in_out.wait()
    sides_sent(act_sides)
    sides_sent(row_sides)
    for k in range(4):
        @pl.when(is_head)
        def _():
            part = qs.at[pl.ds(0, HEADS - 1), k]
            pltpu.make_async_copy(part, part, send_sem.at[4 + k]).wait()

        @pl.when(jnp.logical_not(is_head))
        def _():
            part = qs.at[:, k]
            pltpu.make_async_copy(part, part, send_sem.at[4 + k]).wait()
    part = xr.at[pl.ds(0, PLANE - 1)]
    pltpu.make_async_copy(part, part, send_sem.at[10]).wait()

    @pl.when(is_head)
    def _():
        part = go.at[pl.ds(0, CTX - 1)]
        pltpu.make_async_copy(part, part, send_sem.at[11]).wait()

    part = grr.at[:, pl.ds(0, CHIPS - 1)]
    pltpu.make_async_copy(part, part, send_sem.at[12]).wait()
    for k in range(PARTS):
        pass_on(k).wait_send()
    part = rr.at[pl.ds(0, NZ - 1)]
    pltpu.make_async_copy(part, part, send_sem.at[13]).wait()


def write_out(grad_in_h, grad_conv_h, grad_in_o, grad_conv_o, rows_v, conv_v, in_sem, out_sem):
    step = ROWS // COPIES
    pieces = [pl.ds(i * step, step) for i in range(COPIES)]
    steps = [
        (
            pltpu.make_async_copy(grad_in_h.at[rows, :], rows_v.at[rows, :], in_sem.at[i]),
            pltpu.make_async_copy(rows_v.at[rows, :], grad_in_o.at[rows, :], out_sem.at[i]),
        )
        for i, rows in enumerate(pieces)
    ]
    steps.append(
        (
            pltpu.make_async_copy(grad_conv_h, conv_v, in_sem.at[COPIES]),
            pltpu.make_async_copy(conv_v, grad_conv_o, out_sem.at[COPIES]),
        )
    )
    for load, _ in steps:
        load.start()
    for load, store in steps:
        load.wait()
        store.start()
    for _, store in steps:
        store.wait()


def per_device(
    features, bases, dna_table, norm_gain, w_conv, w_query, w_key, w_value, w_out, cotangent
):
    vmem = pltpu.VMEM
    scratch = [
        vmem((ROWS, C), BF16), vmem((1, ROWS), jnp.int32), vmem((4, C), BF16), vmem((C,), BF16),
        vmem((KW, C, C), BF16), vmem((C, C), BF16), vmem((C, C), BF16), vmem((C, C), BF16),
        vmem((C, C), BF16), vmem((TOK, C), BF16),
        vmem((ROWS, C), BF16),
        vmem((ROWS, C), BF16),
        vmem((ROWS, C), F32),
        vmem((ROWS, 1), F32),
        vmem((ROWS, C), F32),
        vmem((KW * TOK, ROWS), BF16),
        vmem((2, 16, C), BF16),
        vmem((CTX, TOK, XW), BF16),
        vmem((PLANE, TOK, XW), BF16),
        vmem((XW, PLANE * TOK), BF16),
        vmem((HEADS, 4, TOK, DH), BF16),
        vmem((4, SEG_TOK, DH), BF16),
        vmem((SEG_TOK, SEG_TOK), BF16),
        vmem((SEG_TOK, SEG_TOK), BF16),
        vmem((CTX, 3, TOK, DH), BF16),
        vmem((HEADS, 3, TOK, DH), BF16),
        vmem((C, C), BF16),
        vmem((PARTS, 2, TOK, 128), BF16),
        vmem((PARTS, PLANE, TOK, 128), BF16),
        vmem((2, 16, C), BF16),
        vmem((TOK, C), BF16),
        vmem((PARTS, 128, XW), BF16),
        vmem((NZ, PARTS, SUB, XW), BF16),
        vmem((6, TOK, C), F32),
        vmem((ROWS, C), BF16),
        pltpu.SemaphoreType.DMA((11,)),
        pltpu.SemaphoreType.DMA((17,)),
        pltpu.SemaphoreType.DMA((18,)),
    ]
    grad_in, grad_conv = pl.pallas_call(
        body,
        out_shape=(
            jax.ShapeDtypeStruct((ROWS, C), BF16),
            jax.ShapeDtypeStruct((KW, BLK, BLK), F32),
        ),
        in_specs=[pl.BlockSpec(memory_space=pltpu.HBM)] * 10,
        out_specs=(pl.BlockSpec(memory_space=pltpu.HBM), pl.BlockSpec(memory_space=pltpu.VMEM)),
        scratch_shapes=scratch,
        compiler_params=pltpu.CompilerParams(
            collective_id=0, has_side_effects=True, vmem_limit_bytes=56 * 1024 * 1024
        ),
        cost_estimate=pl.CostEstimate(flops=10**9, bytes_accessed=12 * 10**6, transcendentals=10**6),
    )(
        features[0], bases, dna_table, norm_gain, w_conv, w_query, w_key, w_value, w_out,
        cotangent[0],
    )
    grad_in, grad_conv = pl.pallas_call(
        write_out,
        out_shape=(
            jax.ShapeDtypeStruct((ROWS, C), BF16),
            jax.ShapeDtypeStruct((KW, BLK, BLK), F32),
        ),
        in_specs=[pl.BlockSpec(memory_space=pltpu.HBM)] * 2,
        out_specs=(pl.BlockSpec(memory_space=pltpu.HBM),) * 2,
        scratch_shapes=[
            vmem((ROWS, C), BF16), vmem((KW, BLK, BLK), F32),
            pltpu.SemaphoreType.DMA((COPIES + 1,)), pltpu.SemaphoreType.DMA((COPIES + 1,)),
        ],
        compiler_params=pltpu.CompilerParams(vmem_limit_bytes=56 * 1024 * 1024),
    )(grad_in, grad_conv)
    return grad_in[None], grad_conv.transpose(1, 0, 2)


def solution(mesh):
    in_specs = (
        P("dp", "ctx", None),
        P("dp", "ctx"),
        P(),
        P(),
        P(),
        P(),
        P(),
        P(),
        P(),
        P("dp", "ctx", None),
    )
    out_specs = (P("dp", "ctx", None), P("ctx", None, "dp"))
    return jax.shard_map(
        per_device, mesh=mesh, in_specs=in_specs, out_specs=out_specs, check_vma=False
    )
```

```python
import functools

import jax
import jax.numpy as jnp
from jax import lax
from jax.experimental import pallas as pl
from jax.experimental.pallas import tpu as pltpu
from jax.sharding import PartitionSpec as P

HEADS = 6
DH = 128
C = 768
KW = 5
POOL = 16
ROWS = 512
TOK = 32
SEG_TOK = 512
CTX = 16
NZ = 8
PLANE = 32
BLK = 48
PARTS = 3
SUB = 16
COPIES = 4
CHIPS = 16
XW = 256
EPSILON = 1e-06
GELU_SCALE = 0.7978845608028654
CUBIC = 0.044715
MESH = pl.DeviceIdType.MESH
F32 = jnp.float32
BF16 = jnp.bfloat16


PLACE = (0, 2, 4, 8, 12, 14)


def dot(a, b):
    return jnp.dot(a, b, preferred_element_type=F32)


def dot_rt(a, b):
    return lax.dot_general(a, b, (((1,), (1,)), ((), ())), preferred_element_type=F32)


def window_matrix(first, columns):
    row = lax.broadcasted_iota(jnp.int32, (KW * TOK, columns), 0)
    low = (row % TOK) * POOL + row // TOK - 2
    place = lax.broadcasted_iota(jnp.int32, (KW * TOK, columns), 1) + first
    return jnp.where((place >= low) & (place < low + POOL), 1.0, 0.0).astype(BF16)


def body(
    feat_h, base_h, table_h, gain_h, wc_h, wq_h, wk_h, wv_h, wo_h, cot_h,
    grad_in_h, grad_conv_ref,
    feat, base, table, gain, wc, wq, wk, wv, wo, cot,
    emb, act, normed, inv, slope, win, halo, xs, xr, xt,
    qs, hb, pt, gst, go, gb, perm, grp, grr, grh, grs, rs, rr, edge, grad_in_ref,
    in_sem, send_sem, recv_sem,
):
    dp = lax.axis_index("dp")
    ctx = lax.axis_index("ctx")
    zz = dp // 2
    hi = dp % 2
    me = hi * CTX + ctx
    core = ctx % 2
    chip = me // 2
    slot = core * CHIPS + chip
    pair = ctx // 2
    head = pair - pair // 4 - pair // 6
    is_head = (core == 0) & (pair != 3) & (pair != 5)

    def plane_id(p):
        return {"dp": zz * 2 + p // CTX, "ctx": p % CTX}

    def z_id(z):
        return {"dp": z * 2 + hi, "ctx": ctx}

    pairs = [
        (base_h, base), (table_h, table), (gain_h, gain), (feat_h, feat), (cot_h, cot), (wo_h, wo),
        (wc_h, wc), (wq_h, wq), (wk_h, wk), (wv_h, wv),
    ]
    loads = [pltpu.make_async_copy(s, d, in_sem.at[i]) for i, (s, d) in enumerate(pairs)]
    for load in loads:
        load.start()

    barrier = pltpu.get_barrier_semaphore()

    @pl.loop(1, PLANE)
    def _(i):
        pl.semaphore_signal(barrier, inc=1, device_id=plane_id((me + i) % PLANE), device_id_type=MESH)

    @pl.loop(1, NZ)
    def _(i):
        pl.semaphore_signal(barrier, inc=1, device_id=z_id((zz + i) % NZ), device_id_type=MESH)

    win[...] = window_matrix(0, ROWS)
    col = lax.broadcasted_iota(jnp.int32, (C, C), 1)
    group = col // 128
    channel = (2 * (col % 128 // SUB) + group % 2) * BLK + group // 2 * SUB + col % SUB
    perm[...] = jnp.where(channel == lax.broadcasted_iota(jnp.int32, (C, C), 0), 1.0, 0.0).astype(BF16)
    for load in loads[:4]:
        load.wait()

    base_col = jnp.broadcast_to(base[...], (128, ROWS)).T
    onehot = jnp.where(
        base_col == lax.broadcasted_iota(jnp.int32, (ROWS, 128), 1), 1.0, 0.0
    ).astype(BF16)
    row_id = lax.broadcasted_iota(jnp.int32, (128, C), 0)
    tab = jnp.zeros((128, C), F32)
    for b in range(4):
        tab = jnp.where(row_id == b, table[b : b + 1, :].astype(F32), tab)
    tab = tab.astype(BF16)
    emb[...] = dot(onehot, tab).astype(BF16)
    gain_f = gain[...].astype(F32)[None]

    def rows_forward(r0):
        rows = pl.ds(r0, POOL)
        s = feat[rows, :].astype(F32) + emb[rows, :].astype(F32)
        scale = lax.rsqrt(jnp.mean(s * s, axis=-1, keepdims=True) + EPSILON)
        n = s * scale
        u = n * gain_f
        t = jnp.tanh(GELU_SCALE * (u + CUBIC * (u * u * u)))
        act[rows, :] = (0.5 * u * (1.0 + t)).astype(BF16)
        normed[rows, :] = n
        inv[rows, :] = scale

    rows_forward(0)
    rows_forward(ROWS - POOL)
    @pl.loop(1, ROWS // POOL // 2, unroll=3)
    def _(i):
        rows_forward(pl.multiple_of(i * POOL, POOL))

    pl.semaphore_wait(barrier, PLANE - 1 + NZ - 1)

    def sides(first, last, into, sem):
        low = pltpu.make_async_remote_copy(
            src_ref=first, dst_ref=into.at[1], send_sem=send_sem.at[sem], recv_sem=recv_sem.at[sem],
            device_id={"dp": dp, "ctx": jnp.maximum(ctx - 1, 0)}, device_id_type=MESH,
        )
        high = pltpu.make_async_remote_copy(
            src_ref=last, dst_ref=into.at[0], send_sem=send_sem.at[sem + 1], recv_sem=recv_sem.at[sem + 1],
            device_id={"dp": dp, "ctx": jnp.minimum(ctx + 1, CTX - 1)}, device_id_type=MESH,
        )

        @pl.when(ctx > 0)
        def _():
            low.start()

        @pl.when(ctx < CTX - 1)
        def _():
            high.start()

        @pl.when(ctx == 0)
        def _():
            into[0] = jnp.zeros((16, C), BF16)

        @pl.when(ctx == CTX - 1)
        def _():
            into[1] = jnp.zeros((16, C), BF16)

        return low, high

    def sides_arrive(copies):
        low, high = copies

        @pl.when(ctx < CTX - 1)
        def _():
            low.wait_recv()

        @pl.when(ctx > 0)
        def _():
            high.wait_recv()

    def sides_sent(copies):
        low, high = copies

        @pl.when(ctx > 0)
        def _():
            low.wait_send()

        @pl.when(ctx < CTX - 1)
        def _():
            high.wait_send()

    act_sides = sides(act.at[pl.ds(0, 16), :], act.at[pl.ds(ROWS - 16, 16), :], halo, 0)

    @pl.loop(ROWS // POOL // 2, ROWS // POOL - 1, unroll=3)
    def _(i):
        rows_forward(pl.multiple_of(i * POOL, POOL))

    sums = dot(win[...], act[...])
    mean_rows = win[2 * TOK : 3 * TOK, :]
    counts = dot(mean_rows, onehot).astype(BF16)
    pooled_in = dot(mean_rows, feat[...]) + dot(counts, tab)

    loads[4].wait()
    loads[5].wait()
    grad_attn = dot_rt(cot[...], wo[...]).astype(BF16)
    for h in range(HEADS):
        qs[h, 3] = grad_attn[:, h * DH : (h + 1) * DH]

    def to_head(h, k):
        return pltpu.make_async_remote_copy(
            src_ref=qs.at[h, k], dst_ref=hb.at[k, pl.ds(pl.multiple_of(ctx * TOK, TOK), TOK), :],
            send_sem=send_sem.at[4 + k], recv_sem=recv_sem.at[14 + k],
            device_id={"dp": dp, "ctx": PLACE[h]}, device_id_type=MESH,
        )

    def to_heads(k):
        for h in range(HEADS):
            @pl.when(ctx != PLACE[h])
            def _():
                to_head(h, k).start()

    to_heads(3)

    sides_arrive(act_sides)
    edge_win = jnp.concatenate([window_matrix(-16, 16), window_matrix(ROWS, 16)], axis=1)
    sums = sums + dot(edge_win, jnp.concatenate([halo[0], halo[1]], axis=0))
    high_part = sums.astype(BF16)
    low_part = (sums - high_part.astype(F32)).astype(BF16)

    for c in range(CTX):
        cols = [sums[j * TOK : (j + 1) * TOK, c * BLK : (c + 1) * BLK] for j in range(KW)]
        cols.append(jnp.zeros((TOK, XW - KW * BLK), F32))
        xs[c] = jnp.concatenate(cols, axis=1).astype(BF16)

    other = 1 - hi

    def x_send(half, c):
        return pltpu.make_async_remote_copy(
            src_ref=xs.at[c], dst_ref=xr.at[slot], send_sem=send_sem.at[10], recv_sem=recv_sem.at[5],
            device_id={"dp": zz * 2 + half, "ctx": c}, device_id_type=MESH,
        )

    @pl.loop(1, CTX)
    def _(i):
        x_send(hi, (ctx + i) % CTX).start()

    loads[6].wait()
    conv = jnp.zeros((2 * TOK, C), F32)
    for j in range(KW):
        part = slice(j * TOK, (j + 1) * TOK)
        conv = conv + dot(jnp.concatenate([high_part[part], low_part[part]], axis=0), wc[j])
    pooled = ((pooled_in + conv[:TOK] + conv[TOK:]) * (1.0 / POOL)).astype(BF16)

    for i in range(7, 10):
        loads[i].wait()
    for k, weight in ((1, wk), (0, wq), (2, wv)):
        made = dot(pooled, weight[...]).astype(BF16)
        for h in range(HEADS):
            qs[h, k] = made[:, h * DH : (h + 1) * DH]
        to_heads(k)

    def to_other_half():
        @pl.loop(0, CTX)
        def _(i):
            x_send(other, (ctx + i) % CTX).start()

        xr[slot] = xs[ctx]

    def slopes():
        @pl.loop(0, ROWS // POOL, unroll=2)
        def _(i):
            rows = pl.ds(pl.multiple_of(i * POOL, POOL), POOL)
            u = normed[rows, :] * gain_f
            square = u * u
            t = jnp.tanh(GELU_SCALE * (u + CUBIC * (square * u)))
            d = 0.5 * (1.0 + t)
            d = d + 0.5 * u * (1.0 - t * t) * GELU_SCALE * (1.0 + 3.0 * CUBIC * square)
            slope[rows, :] = d * gain_f

    def from_head(c, k):
        return pltpu.make_async_remote_copy(
            src_ref=go.at[c, k], dst_ref=gb.at[head, k],
            send_sem=send_sem.at[11], recv_sem=recv_sem.at[6],
            device_id={"dp": dp, "ctx": c}, device_id_type=MESH,
        )

    def from_heads(k):
        @pl.loop(1, CTX)
        def _(i):
            from_head((ctx + i) % CTX, k).start()

    @pl.when(is_head)
    def _():
        hb[:, pl.ds(pl.multiple_of(ctx * TOK, TOK), TOK), :] = qs[head]
        for k in range(4):
            arrived = hb.at[k, pl.ds(0, SEG_TOK - TOK), :]
            pltpu.make_async_copy(arrived, arrived, recv_sem.at[14 + k]).wait()
        scale = 1.0 / DH**0.5
        keys = hb[1]
        values = hb[2]
        values_t = values.T
        keys_t = keys.T

        @pl.loop(0, SEG_TOK // 128)
        def _(i):
            part = pl.ds(pl.multiple_of(i * 128, 128), 128)
            query = hb[0, part, :]
            grad = hb[3, part, :]
            score = dot_rt(keys, query) * scale
            expo = jnp.exp(score - jnp.max(score, axis=0, keepdims=True))
            prob = expo * (1.0 / jnp.sum(expo, axis=0, keepdims=True))
            prob_b = prob.astype(BF16)
            out_t = dot(values_t, prob_b).astype(BF16).astype(F32)
            delta = jnp.sum(grad.T.astype(F32) * out_t, axis=0, keepdims=True)
            grad_prob = dot_rt(values, grad)
            pt[:, part] = prob_b
            grad_score = (prob * (grad_prob - delta) * scale).astype(BF16)
            gst[:, part] = grad_score
            grad_query = dot(keys_t, grad_score).T.astype(BF16).reshape(4, TOK, DH)
            for m in range(4):
                go[4 * i + m, 0] = grad_query[m]
                @pl.when(ctx != 4 * i + m)
                def _():
                    from_head(4 * i + m, 0).start()

        go[:, 2] = dot(pt[...], hb[3]).astype(BF16).reshape(CTX, TOK, DH)
        from_heads(2)
        go[:, 1] = dot(gst[...], hb[0]).astype(BF16).reshape(CTX, TOK, DH)
        from_heads(1)
        to_other_half()
        gb[head] = go[ctx]
        five = gb.at[pl.ds(0, HEADS - 1)]
        pltpu.make_async_copy(five, five, recv_sem.at[6]).wait()

    @pl.when(jnp.logical_not(is_head))
    def _():
        slopes()
        to_other_half()
        pltpu.make_async_copy(gb, gb, recv_sem.at[6]).wait()

    grad_pooled = cot[...].astype(F32)
    for k, weight in enumerate((wq, wk, wv)):
        whole = jnp.concatenate([gb[h, k] for h in range(HEADS)], axis=1)
        grad_pooled = grad_pooled + dot_rt(whole, weight[...])
    grs[...] = (grad_pooled * (1.0 / POOL)).astype(BF16)
    sorted_g = dot(grs[...], perm[...]).astype(BF16)
    for k in range(PARTS):
        for h in range(2):
            first = (2 * k + h) * 128
            grp[k, h] = sorted_g[:, first : first + 128]

    for k in range(PARTS):
        @pl.loop(1, CHIPS)
        def _(i):
            to = (chip + i) % CHIPS
            pltpu.make_async_remote_copy(
                src_ref=grp.at[k, to // (CHIPS // 2)], dst_ref=grr.at[k, slot],
                send_sem=send_sem.at[12], recv_sem=recv_sem.at[7 + k],
                device_id=plane_id(2 * to + core), device_id_type=MESH,
            ).start()

        grr[k, slot] = grp[k, hi]

    row_sides = sides(grs.at[pl.ds(0, 16), :], grs.at[pl.ds(16, 16), :], grh, 2)

    @pl.when(is_head)
    def _():
        slopes()

    others = xr.at[pl.ds(0, PLANE - 1)]
    pltpu.make_async_copy(others, others, recv_sem.at[5]).wait()
    for i in range(PLANE * TOK // 128):
        block = xr[4 * i : 4 * i + 4].reshape(128, XW)
        xt[:, i * 128 : (i + 1) * 128] = block.T

    factor = 1.0 / (CTX * CTX * ROWS) ** 0.5

    def pass_on(k):
        mine = grr.at[k, pl.ds(pl.multiple_of(core * CHIPS, CHIPS), CHIPS)]
        return pltpu.make_async_remote_copy(
            src_ref=mine, dst_ref=mine, send_sem=send_sem.at[14 + k], recv_sem=recv_sem.at[11 + k],
            device_id={"dp": dp, "ctx": ctx + 1 - 2 * core}, device_id_type=MESH,
        )

    def forward(k):
        others = grr.at[k, pl.ds(0, CHIPS - 1)]
        pltpu.make_async_copy(others, others, recv_sem.at[7 + k]).wait()
        pass_on(k).start()

    def multiply(k):
        pass_on(k).wait_recv()
        made = dot(xt[...], grr[k].reshape(PLANE * TOK, 128)) * factor
        rs[k] = made.T.astype(BF16)

        @pl.loop(1, NZ)
        def _(i):
            z = (zz + i) % NZ
            pltpu.make_async_remote_copy(
                src_ref=rs.at[k, pl.ds(pl.multiple_of(z * SUB, SUB), SUB), :], dst_ref=rr.at[zz, k],
                send_sem=send_sem.at[13], recv_sem=recv_sem.at[10],
                device_id=z_id(z), device_id_type=MESH,
            ).start()

        rr[zz, k] = rs[k, pl.ds(pl.multiple_of(zz * SUB, SUB), SUB), :]

    forward(0)
    forward(1)
    multiply(0)
    forward(2)
    multiply(1)
    multiply(2)

    sides_arrive(row_sides)
    ext = jnp.concatenate([grh[0], grs[...], grh[1]], axis=0)
    first0 = first1 = mid = last0 = last1 = None
    for j in range(KW):
        y = dot_rt(ext, wc[j])
        own, before, after = y[16:48], y[15:47], y[17:49]
        terms = (
            before if j >= 3 else own,
            before if j >= 4 else own,
            own,
            after if j < 1 else own,
            after if j < 2 else own,
        )
        if j == 0:
            first0, first1, mid, last0, last1 = terms
        else:
            first0, first1, mid, last0, last1 = (
                a + b for a, b in zip((first0, first1, mid, last0, last1), terms)
            )
    for k, value in enumerate((first0, first1, mid, last0, last1, grs[...].astype(F32))):
        edge[k] = value

    in_group = lax.broadcasted_iota(jnp.int32, (POOL, C), 0)

    @pl.loop(0, TOK, unroll=2)
    def _(i):
        rows = pl.ds(pl.multiple_of(i * POOL, POOL), POOL)
        one = pl.ds(i, 1)
        g = jnp.broadcast_to(edge[2, one, :], (POOL, C))
        for r, k in ((0, 0), (1, 1), (14, 3), (15, 4)):
            g = jnp.where(in_group == r, edge[k, one, :], g)
        g = g * slope[rows, :]
        n = normed[rows, :]
        mean = jnp.mean(g * n, axis=-1, keepdims=True)
        grad_in_ref[rows, :] = (edge[5, one, :] + inv[rows, :] * (g - n * mean)).astype(BF16)

    grad_in_out = pltpu.make_async_copy(grad_in_ref, grad_in_h, in_sem.at[10])
    grad_in_out.start()

    others = rr.at[pl.ds(0, NZ - 1)]
    pltpu.make_async_copy(others, others, recv_sem.at[10]).wait()
    total = rr[0].astype(F32)
    for z in range(1, NZ):
        total = total + rr[z].astype(F32)
    total = jnp.concatenate([total.reshape(BLK, XW), jnp.zeros((128 - BLK, XW), F32)], axis=0).T
    for j in range(KW):
        grad_conv_ref[j] = total[j * BLK : (j + 1) * BLK, :BLK]

    grad_in_out.wait()
    sides_sent(act_sides)
    sides_sent(row_sides)
    for k in range(4):
        @pl.when(is_head)
        def _():
            part = qs.at[pl.ds(0, HEADS - 1), k]
            pltpu.make_async_copy(part, part, send_sem.at[4 + k]).wait()

        @pl.when(jnp.logical_not(is_head))
        def _():
            part = qs.at[:, k]
            pltpu.make_async_copy(part, part, send_sem.at[4 + k]).wait()
    part = xr.at[pl.ds(0, PLANE - 1)]
    pltpu.make_async_copy(part, part, send_sem.at[10]).wait()

    @pl.when(is_head)
    def _():
        part = go.at[pl.ds(0, CTX - 1)]
        pltpu.make_async_copy(part, part, send_sem.at[11]).wait()

    part = grr.at[:, pl.ds(0, CHIPS - 1)]
    pltpu.make_async_copy(part, part, send_sem.at[12]).wait()
    for k in range(PARTS):
        pass_on(k).wait_send()
    part = rr.at[pl.ds(0, NZ - 1)]
    pltpu.make_async_copy(part, part, send_sem.at[13]).wait()


def write_out(grad_in_h, grad_conv_h, grad_in_o, grad_conv_o, rows_v, conv_v, in_sem, out_sem):
    step = ROWS // COPIES
    pieces = [pl.ds(i * step, step) for i in range(COPIES)]
    steps = [
        (
            pltpu.make_async_copy(grad_in_h.at[rows, :], rows_v.at[rows, :], in_sem.at[i]),
            pltpu.make_async_copy(rows_v.at[rows, :], grad_in_o.at[rows, :], out_sem.at[i]),
        )
        for i, rows in enumerate(pieces)
    ]
    steps.append(
        (
            pltpu.make_async_copy(grad_conv_h, conv_v, in_sem.at[COPIES]),
            pltpu.make_async_copy(conv_v, grad_conv_o, out_sem.at[COPIES]),
        )
    )
    for load, _ in steps:
        load.start()
    for load, store in steps:
        load.wait()
        store.start()
    for _, store in steps:
        store.wait()


def per_device(
    features, bases, dna_table, norm_gain, w_conv, w_query, w_key, w_value, w_out, cotangent
):
    vmem = pltpu.VMEM
    scratch = [
        vmem((ROWS, C), BF16), vmem((1, ROWS), jnp.int32), vmem((4, C), BF16), vmem((C,), BF16),
        vmem((KW, C, C), BF16), vmem((C, C), BF16), vmem((C, C), BF16), vmem((C, C), BF16),
        vmem((C, C), BF16), vmem((TOK, C), BF16),
        vmem((ROWS, C), BF16),
        vmem((ROWS, C), BF16),
        vmem((ROWS, C), F32),
        vmem((ROWS, 1), F32),
        vmem((ROWS, C), F32),
        vmem((KW * TOK, ROWS), BF16),
        vmem((2, 16, C), BF16),
        vmem((CTX, TOK, XW), BF16),
        vmem((PLANE, TOK, XW), BF16),
        vmem((XW, PLANE * TOK), BF16),
        vmem((HEADS, 4, TOK, DH), BF16),
        vmem((4, SEG_TOK, DH), BF16),
        vmem((SEG_TOK, SEG_TOK), BF16),
        vmem((SEG_TOK, SEG_TOK), BF16),
        vmem((CTX, 3, TOK, DH), BF16),
        vmem((HEADS, 3, TOK, DH), BF16),
        vmem((C, C), BF16),
        vmem((PARTS, 2, TOK, 128), BF16),
        vmem((PARTS, PLANE, TOK, 128), BF16),
        vmem((2, 16, C), BF16),
        vmem((TOK, C), BF16),
        vmem((PARTS, 128, XW), BF16),
        vmem((NZ, PARTS, SUB, XW), BF16),
        vmem((6, TOK, C), F32),
        vmem((ROWS, C), BF16),
        pltpu.SemaphoreType.DMA((11,)),
        pltpu.SemaphoreType.DMA((17,)),
        pltpu.SemaphoreType.DMA((18,)),
    ]
    grad_in, grad_conv = pl.pallas_call(
        body,
        out_shape=(
            jax.ShapeDtypeStruct((ROWS, C), BF16),
            jax.ShapeDtypeStruct((KW, BLK, BLK), F32),
        ),
        in_specs=[pl.BlockSpec(memory_space=pltpu.HBM)] * 10,
        out_specs=(pl.BlockSpec(memory_space=pltpu.HBM), pl.BlockSpec(memory_space=pltpu.VMEM)),
        scratch_shapes=scratch,
        compiler_params=pltpu.CompilerParams(
            collective_id=0, has_side_effects=True, vmem_limit_bytes=56 * 1024 * 1024
        ),
        cost_estimate=pl.CostEstimate(flops=10**9, bytes_accessed=12 * 10**6, transcendentals=10**6),
    )(
        features[0], bases, dna_table, norm_gain, w_conv, w_query, w_key, w_value, w_out,
        cotangent[0],
    )
    grad_in, grad_conv = pl.pallas_call(
        write_out,
        out_shape=(
            jax.ShapeDtypeStruct((ROWS, C), BF16),
            jax.ShapeDtypeStruct((KW, BLK, BLK), F32),
        ),
        in_specs=[pl.BlockSpec(memory_space=pltpu.HBM)] * 2,
        out_specs=(pl.BlockSpec(memory_space=pltpu.HBM),) * 2,
        scratch_shapes=[
            vmem((ROWS, C), BF16), vmem((KW, BLK, BLK), F32),
            pltpu.SemaphoreType.DMA((COPIES + 1,)), pltpu.SemaphoreType.DMA((COPIES + 1,)),
        ],
        compiler_params=pltpu.CompilerParams(vmem_limit_bytes=56 * 1024 * 1024),
    )(grad_in, grad_conv)
    return grad_in[None], grad_conv.transpose(1, 0, 2)


def solution(mesh):
    in_specs = (
        P("dp", "ctx", None),
        P("dp", "ctx"),
        P(),
        P(),
        P(),
        P(),
        P(),
        P(),
        P(),
        P("dp", "ctx", None),
    )
    out_specs = (P("dp", "ctx", None), P("ctx", None, "dp"))
    return jax.shard_map(
        per_device, mesh=mesh, in_specs=in_specs, out_specs=out_specs, check_vma=False
    )
```

```python
import functools

import jax
import jax.numpy as jnp
from jax import lax
from jax.experimental import pallas as pl
from jax.experimental.pallas import tpu as pltpu
from jax.sharding import PartitionSpec as P

HEADS = 6
DH = 128
C = 768
KW = 5
POOL = 16
ROWS = 512
TOK = 32
SEG_TOK = 512
CTX = 16
NZ = 8
PLANE = 32
BLK = 48
PARTS = 3
SUB = 16
COPIES = 2
CHIPS = 16
XW = 256
EPSILON = 1e-06
GELU_SCALE = 0.7978845608028654
CUBIC = 0.044715
MESH = pl.DeviceIdType.MESH
F32 = jnp.float32
BF16 = jnp.bfloat16


PLACE = (0, 2, 4, 8, 12, 14)


FAR_FIRST = sorted(
    [(dx, dy) for dx in range(4) for dy in range(4) if dx or dy],
    key=lambda d: -(min(d[0], 4 - d[0]) + min(d[1], 4 - d[1])),
)


def dot(a, b):
    return jnp.dot(a, b, preferred_element_type=F32)


def dot_rt(a, b):
    return lax.dot_general(a, b, (((1,), (1,)), ((), ())), preferred_element_type=F32)


def window_matrix(first, columns):
    row = lax.broadcasted_iota(jnp.int32, (KW * TOK, columns), 0)
    low = (row % TOK) * POOL + row // TOK - 2
    place = lax.broadcasted_iota(jnp.int32, (KW * TOK, columns), 1) + first
    return jnp.where((place >= low) & (place < low + POOL), 1.0, 0.0).astype(BF16)


def body(
    feat_h, base_h, table_h, gain_h, wc_h, wq_h, wk_h, wv_h, wo_h, cot_h,
    grad_in_h, grad_conv_ref,
    feat, base, table, gain, wc, wq, wk, wv, wo, cot,
    emb, act, normed, inv, slope, win, halo, xs, xr, xt,
    qs, hb, pt, gst, go, gb, perm, grp, grr, grh, grs, rs, rr, edge, grad_in_ref,
    in_sem, send_sem, recv_sem,
):
    dp = lax.axis_index("dp")
    ctx = lax.axis_index("ctx")
    zz = dp // 2
    hi = dp % 2
    me = hi * CTX + ctx
    core = ctx % 2
    chip = me // 2
    slot = core * CHIPS + chip
    pair = ctx // 2
    head = pair - pair // 4 - pair // 6
    is_head = (core == 0) & (pair != 3) & (pair != 5)

    def plane_id(p):
        return {"dp": zz * 2 + p // CTX, "ctx": p % CTX}

    def z_id(z):
        return {"dp": z * 2 + hi, "ctx": ctx}

    pairs = [
        (base_h, base), (table_h, table), (gain_h, gain), (feat_h, feat), (cot_h, cot), (wo_h, wo),
        (wc_h, wc), (wq_h, wq), (wk_h, wk), (wv_h, wv),
    ]
    loads = [pltpu.make_async_copy(s, d, in_sem.at[i]) for i, (s, d) in enumerate(pairs)]
    for load in loads:
        load.start()

    barrier = pltpu.get_barrier_semaphore()

    @pl.loop(1, PLANE)
    def _(i):
        pl.semaphore_signal(barrier, inc=1, device_id=plane_id((me + i) % PLANE), device_id_type=MESH)

    @pl.loop(1, NZ)
    def _(i):
        pl.semaphore_signal(barrier, inc=1, device_id=z_id((zz + i) % NZ), device_id_type=MESH)

    win[...] = window_matrix(0, ROWS)
    col = lax.broadcasted_iota(jnp.int32, (C, C), 1)
    group = col // 128
    channel = (2 * (col % 128 // SUB) + group % 2) * BLK + group // 2 * SUB + col % SUB
    perm[...] = jnp.where(channel == lax.broadcasted_iota(jnp.int32, (C, C), 0), 1.0, 0.0).astype(BF16)
    for load in loads[:4]:
        load.wait()

    base_col = jnp.broadcast_to(base[...], (128, ROWS)).T
    onehot = jnp.where(
        base_col == lax.broadcasted_iota(jnp.int32, (ROWS, 128), 1), 1.0, 0.0
    ).astype(BF16)
    row_id = lax.broadcasted_iota(jnp.int32, (128, C), 0)
    tab = jnp.zeros((128, C), F32)
    for b in range(4):
        tab = jnp.where(row_id == b, table[b : b + 1, :].astype(F32), tab)
    tab = tab.astype(BF16)
    emb[...] = dot(onehot, tab).astype(BF16)
    gain_f = gain[...].astype(F32)[None]

    def rows_forward(r0):
        rows = pl.ds(r0, POOL)
        s = feat[rows, :].astype(F32) + emb[rows, :].astype(F32)
        scale = lax.rsqrt(jnp.mean(s * s, axis=-1, keepdims=True) + EPSILON)
        n = s * scale
        u = n * gain_f
        t = jnp.tanh(GELU_SCALE * (u + CUBIC * (u * u * u)))
        act[rows, :] = (0.5 * u * (1.0 + t)).astype(BF16)
        normed[rows, :] = n
        inv[rows, :] = scale

    rows_forward(0)
    rows_forward(ROWS - POOL)
    @pl.loop(1, ROWS // POOL // 2, unroll=3)
    def _(i):
        rows_forward(pl.multiple_of(i * POOL, POOL))

    pl.semaphore_wait(barrier, PLANE - 1 + NZ - 1)

    def sides(first, last, into, sem):
        low = pltpu.make_async_remote_copy(
            src_ref=first, dst_ref=into.at[1], send_sem=send_sem.at[sem], recv_sem=recv_sem.at[sem],
            device_id={"dp": dp, "ctx": jnp.maximum(ctx - 1, 0)}, device_id_type=MESH,
        )
        high = pltpu.make_async_remote_copy(
            src_ref=last, dst_ref=into.at[0], send_sem=send_sem.at[sem + 1], recv_sem=recv_sem.at[sem + 1],
            device_id={"dp": dp, "ctx": jnp.minimum(ctx + 1, CTX - 1)}, device_id_type=MESH,
        )

        @pl.when(ctx > 0)
        def _():
            low.start()

        @pl.when(ctx < CTX - 1)
        def _():
            high.start()

        @pl.when(ctx == 0)
        def _():
            into[0] = jnp.zeros((16, C), BF16)

        @pl.when(ctx == CTX - 1)
        def _():
            into[1] = jnp.zeros((16, C), BF16)

        return low, high

    def sides_arrive(copies):
        low, high = copies

        @pl.when(ctx < CTX - 1)
        def _():
            low.wait_recv()

        @pl.when(ctx > 0)
        def _():
            high.wait_recv()

    def sides_sent(copies):
        low, high = copies

        @pl.when(ctx > 0)
        def _():
            low.wait_send()

        @pl.when(ctx < CTX - 1)
        def _():
            high.wait_send()

    act_sides = sides(act.at[pl.ds(0, 16), :], act.at[pl.ds(ROWS - 16, 16), :], halo, 0)

    @pl.loop(ROWS // POOL // 2, ROWS // POOL - 1, unroll=3)
    def _(i):
        rows_forward(pl.multiple_of(i * POOL, POOL))

    sums = dot(win[...], act[...])
    mean_rows = win[2 * TOK : 3 * TOK, :]
    counts = dot(mean_rows, onehot).astype(BF16)
    pooled_in = dot(mean_rows, feat[...]) + dot(counts, tab)

    loads[4].wait()
    loads[5].wait()
    grad_attn = dot_rt(cot[...], wo[...]).astype(BF16)
    for h in range(HEADS):
        qs[h, 3] = grad_attn[:, h * DH : (h + 1) * DH]

    def to_head(h, k):
        return pltpu.make_async_remote_copy(
            src_ref=qs.at[h, k], dst_ref=hb.at[k, pl.ds(pl.multiple_of(ctx * TOK, TOK), TOK), :],
            send_sem=send_sem.at[4 + k], recv_sem=recv_sem.at[14 + k],
            device_id={"dp": dp, "ctx": PLACE[h]}, device_id_type=MESH,
        )

    def to_heads(k):
        for h in range(HEADS):
            @pl.when(ctx != PLACE[h])
            def _():
                to_head(h, k).start()

    to_heads(3)

    sides_arrive(act_sides)
    edge_win = jnp.concatenate([window_matrix(-16, 16), window_matrix(ROWS, 16)], axis=1)
    sums = sums + dot(edge_win, jnp.concatenate([halo[0], halo[1]], axis=0))
    high_part = sums.astype(BF16)
    low_part = (sums - high_part.astype(F32)).astype(BF16)

    for c in range(CTX):
        cols = [high_part[j * TOK : (j + 1) * TOK, c * BLK : (c + 1) * BLK] for j in range(KW)]
        cols.append(jnp.zeros((TOK, XW - KW * BLK), BF16))
        xs[c] = jnp.concatenate(cols, axis=1)

    other = 1 - hi

    def x_send(half, c):
        return pltpu.make_async_remote_copy(
            src_ref=xs.at[c], dst_ref=xr.at[slot], send_sem=send_sem.at[10], recv_sem=recv_sem.at[5],
            device_id={"dp": zz * 2 + half, "ctx": c}, device_id_type=MESH,
        )

    @pl.loop(1, CTX)
    def _(i):
        x_send(hi, (ctx + i) % CTX).start()

    loads[6].wait()
    conv = jnp.zeros((2 * TOK, C), F32)
    for j in range(KW):
        part = slice(j * TOK, (j + 1) * TOK)
        conv = conv + dot(jnp.concatenate([high_part[part], low_part[part]], axis=0), wc[j])
    pooled = ((pooled_in + conv[:TOK] + conv[TOK:]) * (1.0 / POOL)).astype(BF16)

    for i in range(7, 10):
        loads[i].wait()
    for k, weight in ((1, wk), (0, wq), (2, wv)):
        made = dot(pooled, weight[...]).astype(BF16)
        for h in range(HEADS):
            qs[h, k] = made[:, h * DH : (h + 1) * DH]
        to_heads(k)

    def to_other_half():
        @pl.loop(0, CTX)
        def _(i):
            x_send(other, (ctx + i) % CTX).start()

        xr[slot] = xs[ctx]

    def slopes():
        @pl.loop(0, ROWS // POOL, unroll=2)
        def _(i):
            rows = pl.ds(pl.multiple_of(i * POOL, POOL), POOL)
            u = normed[rows, :] * gain_f
            square = u * u
            t = jnp.tanh(GELU_SCALE * (u + CUBIC * (square * u)))
            d = 0.5 * (1.0 + t)
            d = d + 0.5 * u * (1.0 - t * t) * GELU_SCALE * (1.0 + 3.0 * CUBIC * square)
            slope[rows, :] = d * gain_f

    def from_head(c, k):
        return pltpu.make_async_remote_copy(
            src_ref=go.at[c, k], dst_ref=gb.at[head, k],
            send_sem=send_sem.at[11], recv_sem=recv_sem.at[6],
            device_id={"dp": dp, "ctx": c}, device_id_type=MESH,
        )

    def from_heads(k):
        @pl.loop(1, CTX)
        def _(i):
            from_head((ctx + i) % CTX, k).start()

    @pl.when(is_head)
    def _():
        hb[:, pl.ds(pl.multiple_of(ctx * TOK, TOK), TOK), :] = qs[head]
        for k in range(4):
            arrived = hb.at[k, pl.ds(0, SEG_TOK - TOK), :]
            pltpu.make_async_copy(arrived, arrived, recv_sem.at[14 + k]).wait()
        scale = 1.0 / DH**0.5
        keys = hb[1]
        values = hb[2]
        values_t = values.T
        keys_t = keys.T

        @pl.loop(0, SEG_TOK // 128)
        def _(i):
            part = pl.ds(pl.multiple_of(i * 128, 128), 128)
            query = hb[0, part, :]
            grad = hb[3, part, :]
            score = dot_rt(keys, query) * scale
            expo = jnp.exp(score - jnp.max(score, axis=0, keepdims=True))
            prob = expo * (1.0 / jnp.sum(expo, axis=0, keepdims=True))
            prob_b = prob.astype(BF16)
            out_t = dot(values_t, prob_b).astype(BF16).astype(F32)
            delta = jnp.sum(grad.T.astype(F32) * out_t, axis=0, keepdims=True)
            grad_prob = dot_rt(values, grad)
            pt[:, part] = prob_b
            grad_score = (prob * (grad_prob - delta) * scale).astype(BF16)
            gst[:, part] = grad_score
            grad_query = dot(keys_t, grad_score).T.astype(BF16).reshape(4, TOK, DH)
            for m in range(4):
                go[4 * i + m, 0] = grad_query[m]
                @pl.when(ctx != 4 * i + m)
                def _():
                    from_head(4 * i + m, 0).start()

        go[:, 2] = dot(pt[...], hb[3]).astype(BF16).reshape(CTX, TOK, DH)
        from_heads(2)
        go[:, 1] = dot(gst[...], hb[0]).astype(BF16).reshape(CTX, TOK, DH)
        from_heads(1)
        to_other_half()
        gb[head] = go[ctx]
        five = gb.at[pl.ds(0, HEADS - 1)]
        pltpu.make_async_copy(five, five, recv_sem.at[6]).wait()

    @pl.when(jnp.logical_not(is_head))
    def _():
        slopes()
        to_other_half()
        pltpu.make_async_copy(gb, gb, recv_sem.at[6]).wait()

    grad_pooled = cot[...].astype(F32)
    for k, weight in enumerate((wq, wk, wv)):
        whole = jnp.concatenate([gb[h, k] for h in range(HEADS)], axis=1)
        grad_pooled = grad_pooled + dot_rt(whole, weight[...])
    grs[...] = (grad_pooled * (1.0 / POOL)).astype(BF16)
    sorted_g = dot(grs[...], perm[...]).astype(BF16)
    for k in range(PARTS):
        for h in range(2):
            first = (2 * k + h) * 128
            grp[k, h] = sorted_g[:, first : first + 128]

    for k in range(PARTS):
        for dx, dy in FAR_FIRST:
            to = (chip // 4 + dx) % 4 * 4 + (chip + dy) % 4
            pltpu.make_async_remote_copy(
                src_ref=grp.at[k, to // (CHIPS // 2)], dst_ref=grr.at[k, slot],
                send_sem=send_sem.at[12], recv_sem=recv_sem.at[7 + k],
                device_id=plane_id(2 * to + core), device_id_type=MESH,
            ).start()

        grr[k, slot] = grp[k, hi]

    row_sides = sides(grs.at[pl.ds(0, 16), :], grs.at[pl.ds(16, 16), :], grh, 2)

    @pl.when(is_head)
    def _():
        slopes()

    others = xr.at[pl.ds(0, PLANE - 1)]
    pltpu.make_async_copy(others, others, recv_sem.at[5]).wait()
    for i in range(PLANE * TOK // 128):
        block = xr[4 * i : 4 * i + 4].reshape(128, XW)
        xt[:, i * 128 : (i + 1) * 128] = block.T

    factor = 1.0 / (CTX * CTX * ROWS) ** 0.5

    def pass_on(k):
        mine = grr.at[k, pl.ds(pl.multiple_of(core * CHIPS, CHIPS), CHIPS)]
        return pltpu.make_async_remote_copy(
            src_ref=mine, dst_ref=mine, send_sem=send_sem.at[14 + k], recv_sem=recv_sem.at[11 + k],
            device_id={"dp": dp, "ctx": ctx + 1 - 2 * core}, device_id_type=MESH,
        )

    def forward(k):
        others = grr.at[k, pl.ds(0, CHIPS - 1)]
        pltpu.make_async_copy(others, others, recv_sem.at[7 + k]).wait()
        pass_on(k).start()

    def multiply(k):
        pass_on(k).wait_recv()
        made = dot(xt[...], grr[k].reshape(PLANE * TOK, 128)) * factor
        rs[k] = made.T.astype(BF16)

        for i in (4, 3, 5, 2, 6, 1, 7):
            z = (zz + i) % NZ
            pltpu.make_async_remote_copy(
                src_ref=rs.at[k, pl.ds(pl.multiple_of(z * SUB, SUB), SUB), :], dst_ref=rr.at[zz, k],
                send_sem=send_sem.at[13], recv_sem=recv_sem.at[10],
                device_id=z_id(z), device_id_type=MESH,
            ).start()

        rr[zz, k] = rs[k, pl.ds(pl.multiple_of(zz * SUB, SUB), SUB), :]

    forward(0)
    forward(1)
    multiply(0)
    forward(2)
    multiply(1)
    multiply(2)

    sides_arrive(row_sides)
    ext = jnp.concatenate([grh[0], grs[...], grh[1]], axis=0)
    first0 = first1 = mid = last0 = last1 = None
    for j in range(KW):
        y = dot_rt(ext, wc[j])
        own, before, after = y[16:48], y[15:47], y[17:49]
        terms = (
            before if j >= 3 else own,
            before if j >= 4 else own,
            own,
            after if j < 1 else own,
            after if j < 2 else own,
        )
        if j == 0:
            first0, first1, mid, last0, last1 = terms
        else:
            first0, first1, mid, last0, last1 = (
                a + b for a, b in zip((first0, first1, mid, last0, last1), terms)
            )
    for k, value in enumerate((first0, first1, mid, last0, last1, grs[...].astype(F32))):
        edge[k] = value

    in_group = lax.broadcasted_iota(jnp.int32, (POOL, C), 0)

    @pl.loop(0, TOK, unroll=2)
    def _(i):
        rows = pl.ds(pl.multiple_of(i * POOL, POOL), POOL)
        one = pl.ds(i, 1)
        g = jnp.broadcast_to(edge[2, one, :], (POOL, C))
        for r, k in ((0, 0), (1, 1), (14, 3), (15, 4)):
            g = jnp.where(in_group == r, edge[k, one, :], g)
        g = g * slope[rows, :]
        n = normed[rows, :]
        mean = jnp.mean(g * n, axis=-1, keepdims=True)
        grad_in_ref[rows, :] = (edge[5, one, :] + inv[rows, :] * (g - n * mean)).astype(BF16)

    grad_in_out = pltpu.make_async_copy(grad_in_ref, grad_in_h, in_sem.at[10])
    grad_in_out.start()

    others = rr.at[pl.ds(0, NZ - 1)]
    pltpu.make_async_copy(others, others, recv_sem.at[10]).wait()
    total = rr[0].astype(F32)
    for z in range(1, NZ):
        total = total + rr[z].astype(F32)
    total = jnp.concatenate([total.reshape(BLK, XW), jnp.zeros((128 - BLK, XW), F32)], axis=0).T
    for j in range(KW):
        grad_conv_ref[j] = total[j * BLK : (j + 1) * BLK, :BLK]

    grad_in_out.wait()
    sides_sent(act_sides)
    sides_sent(row_sides)
    for k in range(4):
        @pl.when(is_head)
        def _():
            part = qs.at[pl.ds(0, HEADS - 1), k]
            pltpu.make_async_copy(part, part, send_sem.at[4 + k]).wait()

        @pl.when(jnp.logical_not(is_head))
        def _():
            part = qs.at[:, k]
            pltpu.make_async_copy(part, part, send_sem.at[4 + k]).wait()
    part = xr.at[pl.ds(0, PLANE - 1)]
    pltpu.make_async_copy(part, part, send_sem.at[10]).wait()

    @pl.when(is_head)
    def _():
        part = go.at[pl.ds(0, CTX - 1)]
        pltpu.make_async_copy(part, part, send_sem.at[11]).wait()

    part = grr.at[:, pl.ds(0, CHIPS - 1)]
    pltpu.make_async_copy(part, part, send_sem.at[12]).wait()
    for k in range(PARTS):
        pass_on(k).wait_send()
    part = rr.at[pl.ds(0, NZ - 1)]
    pltpu.make_async_copy(part, part, send_sem.at[13]).wait()


def write_out(grad_in_h, grad_conv_h, grad_in_o, grad_conv_o, rows_v, conv_v, in_sem, out_sem):
    step = ROWS // COPIES
    pieces = [pl.ds(i * step, step) for i in range(COPIES)]
    steps = [
        (
            pltpu.make_async_copy(grad_in_h.at[rows, :], rows_v.at[rows, :], in_sem.at[i]),
            pltpu.make_async_copy(rows_v.at[rows, :], grad_in_o.at[rows, :], out_sem.at[i]),
        )
        for i, rows in enumerate(pieces)
    ]
    steps.append(
        (
            pltpu.make_async_copy(grad_conv_h, conv_v, in_sem.at[COPIES]),
            pltpu.make_async_copy(conv_v, grad_conv_o, out_sem.at[COPIES]),
        )
    )
    for load, _ in steps:
        load.start()
    for load, store in steps:
        load.wait()
        store.start()
    for _, store in steps:
        store.wait()


def per_device(
    features, bases, dna_table, norm_gain, w_conv, w_query, w_key, w_value, w_out, cotangent
):
    vmem = pltpu.VMEM
    scratch = [
        vmem((ROWS, C), BF16), vmem((1, ROWS), jnp.int32), vmem((4, C), BF16), vmem((C,), BF16),
        vmem((KW, C, C), BF16), vmem((C, C), BF16), vmem((C, C), BF16), vmem((C, C), BF16),
        vmem((C, C), BF16), vmem((TOK, C), BF16),
        vmem((ROWS, C), BF16),
        vmem((ROWS, C), BF16),
        vmem((ROWS, C), F32),
        vmem((ROWS, 1), F32),
        vmem((ROWS, C), F32),
        vmem((KW * TOK, ROWS), BF16),
        vmem((2, 16, C), BF16),
        vmem((CTX, TOK, XW), BF16),
        vmem((PLANE, TOK, XW), BF16),
        vmem((XW, PLANE * TOK), BF16),
        vmem((HEADS, 4, TOK, DH), BF16),
        vmem((4, SEG_TOK, DH), BF16),
        vmem((SEG_TOK, SEG_TOK), BF16),
        vmem((SEG_TOK, SEG_TOK), BF16),
        vmem((CTX, 3, TOK, DH), BF16),
        vmem((HEADS, 3, TOK, DH), BF16),
        vmem((C, C), BF16),
        vmem((PARTS, 2, TOK, 128), BF16),
        vmem((PARTS, PLANE, TOK, 128), BF16),
        vmem((2, 16, C), BF16),
        vmem((TOK, C), BF16),
        vmem((PARTS, 128, XW), BF16),
        vmem((NZ, PARTS, SUB, XW), BF16),
        vmem((6, TOK, C), F32),
        vmem((ROWS, C), BF16),
        pltpu.SemaphoreType.DMA((11,)),
        pltpu.SemaphoreType.DMA((17,)),
        pltpu.SemaphoreType.DMA((18,)),
    ]
    grad_in, grad_conv = pl.pallas_call(
        body,
        out_shape=(
            jax.ShapeDtypeStruct((ROWS, C), BF16),
            jax.ShapeDtypeStruct((KW, BLK, BLK), F32),
        ),
        in_specs=[pl.BlockSpec(memory_space=pltpu.HBM)] * 10,
        out_specs=(pl.BlockSpec(memory_space=pltpu.HBM), pl.BlockSpec(memory_space=pltpu.VMEM)),
        scratch_shapes=scratch,
        compiler_params=pltpu.CompilerParams(
            collective_id=0, has_side_effects=True, vmem_limit_bytes=56 * 1024 * 1024
        ),
        cost_estimate=pl.CostEstimate(flops=10**9, bytes_accessed=12 * 10**6, transcendentals=10**6),
    )(
        features[0], bases, dna_table, norm_gain, w_conv, w_query, w_key, w_value, w_out,
        cotangent[0],
    )
    grad_in, grad_conv = pl.pallas_call(
        write_out,
        out_shape=(
            jax.ShapeDtypeStruct((ROWS, C), BF16),
            jax.ShapeDtypeStruct((KW, BLK, BLK), F32),
        ),
        in_specs=[pl.BlockSpec(memory_space=pltpu.HBM)] * 2,
        out_specs=(pl.BlockSpec(memory_space=pltpu.HBM),) * 2,
        scratch_shapes=[
            vmem((ROWS, C), BF16), vmem((KW, BLK, BLK), F32),
            pltpu.SemaphoreType.DMA((COPIES + 1,)), pltpu.SemaphoreType.DMA((COPIES + 1,)),
        ],
        compiler_params=pltpu.CompilerParams(vmem_limit_bytes=56 * 1024 * 1024),
    )(grad_in, grad_conv)
    return grad_in[None], grad_conv.transpose(1, 0, 2)


def solution(mesh):
    in_specs = (
        P("dp", "ctx", None),
        P("dp", "ctx"),
        P(),
        P(),
        P(),
        P(),
        P(),
        P(),
        P(),
        P("dp", "ctx", None),
    )
    out_specs = (P("dp", "ctx", None), P("ctx", None, "dp"))
    return jax.shard_map(
        per_device, mesh=mesh, in_specs=in_specs, out_specs=out_specs, check_vma=False
    )
```

```python
import functools

import jax
import jax.numpy as jnp
from jax import lax
from jax.experimental import pallas as pl
from jax.experimental.pallas import tpu as pltpu
from jax.sharding import PartitionSpec as P

HEADS = 6
DH = 128
C = 768
KW = 5
POOL = 16
ROWS = 512
TOK = 32
SEG_TOK = 512
CTX = 16
NZ = 8
PLANE = 32
BLK = 48
PARTS = 3
SUB = 16
COPIES = 2
CHIPS = 16
XW = 256
EPSILON = 1e-06
GELU_SCALE = 0.7978845608028654
CUBIC = 0.044715
MESH = pl.DeviceIdType.MESH
F32 = jnp.float32
BF16 = jnp.bfloat16


PLACE = (0, 2, 4, 8, 12, 14)


FAR_FIRST = sorted(
    [(dx, dy) for dx in range(4) for dy in range(4) if dx or dy],
    key=lambda d: -(min(d[0], 4 - d[0]) + min(d[1], 4 - d[1])),
)

SEGMENT_FAR_FIRST = sorted(
    [(dx, dy, dc) for dx in range(2) for dy in range(4) for dc in range(2) if dx or dy or dc],
    key=lambda d: -(d[0] + min(d[1], 4 - d[1])),
)


def dot(a, b):
    return jnp.dot(a, b, preferred_element_type=F32)


def dot_rt(a, b):
    return lax.dot_general(a, b, (((1,), (1,)), ((), ())), preferred_element_type=F32)


def window_matrix(first, columns):
    row = lax.broadcasted_iota(jnp.int32, (KW * TOK, columns), 0)
    low = (row % TOK) * POOL + row // TOK - 2
    place = lax.broadcasted_iota(jnp.int32, (KW * TOK, columns), 1) + first
    return jnp.where((place >= low) & (place < low + POOL), 1.0, 0.0).astype(BF16)


def body(
    feat_h, base_h, table_h, gain_h, wc_h, wq_h, wk_h, wv_h, wo_h, cot_h,
    grad_in_h, grad_conv_ref,
    feat, base, table, gain, wc, wq, wk, wv, wo, cot,
    emb, act, normed, inv, slope, win, halo, xs, xr, xt,
    qs, hb, pt, gst, go, gb, perm, grp, grr, grh, grs, rs, rr, edge, grad_in_ref,
    in_sem, send_sem, recv_sem,
):
    dp = lax.axis_index("dp")
    ctx = lax.axis_index("ctx")
    zz = dp // 2
    hi = dp % 2
    me = hi * CTX + ctx
    core = ctx % 2
    chip = me // 2
    slot = core * CHIPS + chip
    pair = ctx // 2
    head = pair - pair // 4 - pair // 6
    is_head = (core == 0) & (pair != 3) & (pair != 5)

    def plane_id(p):
        return {"dp": zz * 2 + p // CTX, "ctx": p % CTX}

    def z_id(z):
        return {"dp": z * 2 + hi, "ctx": ctx}

    pairs = [
        (base_h, base), (table_h, table), (gain_h, gain), (feat_h, feat), (cot_h, cot), (wo_h, wo),
        (wc_h, wc), (wq_h, wq), (wk_h, wk), (wv_h, wv),
    ]
    loads = [pltpu.make_async_copy(s, d, in_sem.at[i]) for i, (s, d) in enumerate(pairs)]
    for load in loads:
        load.start()

    barrier = pltpu.get_barrier_semaphore()

    @pl.loop(1, PLANE)
    def _(i):
        pl.semaphore_signal(barrier, inc=1, device_id=plane_id((me + i) % PLANE), device_id_type=MESH)

    @pl.loop(1, NZ)
    def _(i):
        pl.semaphore_signal(barrier, inc=1, device_id=z_id((zz + i) % NZ), device_id_type=MESH)

    win[...] = window_matrix(0, ROWS)
    col = lax.broadcasted_iota(jnp.int32, (C, C), 1)
    group = col // 128
    channel = (2 * (col % 128 // SUB) + group % 2) * BLK + group // 2 * SUB + col % SUB
    perm[...] = jnp.where(channel == lax.broadcasted_iota(jnp.int32, (C, C), 0), 1.0, 0.0).astype(BF16)
    for load in loads[:4]:
        load.wait()

    base_col = jnp.broadcast_to(base[...], (128, ROWS)).T
    onehot = jnp.where(
        base_col == lax.broadcasted_iota(jnp.int32, (ROWS, 128), 1), 1.0, 0.0
    ).astype(BF16)
    row_id = lax.broadcasted_iota(jnp.int32, (128, C), 0)
    tab = jnp.zeros((128, C), F32)
    for b in range(4):
        tab = jnp.where(row_id == b, table[b : b + 1, :].astype(F32), tab)
    tab = tab.astype(BF16)
    emb[...] = dot(onehot, tab).astype(BF16)
    gain_f = gain[...].astype(F32)[None]

    def rows_forward(r0):
        rows = pl.ds(r0, POOL)
        s = feat[rows, :].astype(F32) + emb[rows, :].astype(F32)
        scale = lax.rsqrt(jnp.mean(s * s, axis=-1, keepdims=True) + EPSILON)
        n = s * scale
        u = n * gain_f
        t = jnp.tanh(GELU_SCALE * (u + CUBIC * (u * u * u)))
        act[rows, :] = (0.5 * u * (1.0 + t)).astype(BF16)
        normed[rows, :] = n
        inv[rows, :] = scale

    rows_forward(0)
    rows_forward(ROWS - POOL)
    @pl.loop(1, ROWS // POOL // 2, unroll=3)
    def _(i):
        rows_forward(pl.multiple_of(i * POOL, POOL))

    pl.semaphore_wait(barrier, PLANE - 1 + NZ - 1)

    def sides(first, last, into, sem):
        low = pltpu.make_async_remote_copy(
            src_ref=first, dst_ref=into.at[1], send_sem=send_sem.at[sem], recv_sem=recv_sem.at[sem],
            device_id={"dp": dp, "ctx": jnp.maximum(ctx - 1, 0)}, device_id_type=MESH,
        )
        high = pltpu.make_async_remote_copy(
            src_ref=last, dst_ref=into.at[0], send_sem=send_sem.at[sem + 1], recv_sem=recv_sem.at[sem + 1],
            device_id={"dp": dp, "ctx": jnp.minimum(ctx + 1, CTX - 1)}, device_id_type=MESH,
        )

        @pl.when(ctx > 0)
        def _():
            low.start()

        @pl.when(ctx < CTX - 1)
        def _():
            high.start()

        @pl.when(ctx == 0)
        def _():
            into[0] = jnp.zeros((16, C), BF16)

        @pl.when(ctx == CTX - 1)
        def _():
            into[1] = jnp.zeros((16, C), BF16)

        return low, high

    def sides_arrive(copies):
        low, high = copies

        @pl.when(ctx < CTX - 1)
        def _():
            low.wait_recv()

        @pl.when(ctx > 0)
        def _():
            high.wait_recv()

    def sides_sent(copies):
        low, high = copies

        @pl.when(ctx > 0)
        def _():
            low.wait_send()

        @pl.when(ctx < CTX - 1)
        def _():
            high.wait_send()

    act_sides = sides(act.at[pl.ds(0, 16), :], act.at[pl.ds(ROWS - 16, 16), :], halo, 0)

    @pl.loop(ROWS // POOL // 2, ROWS // POOL - 1, unroll=3)
    def _(i):
        rows_forward(pl.multiple_of(i * POOL, POOL))

    sums = dot(win[...], act[...])
    mean_rows = win[2 * TOK : 3 * TOK, :]
    counts = dot(mean_rows, onehot).astype(BF16)
    pooled_in = dot(mean_rows, feat[...]) + dot(counts, tab)

    loads[4].wait()
    loads[5].wait()
    grad_attn = dot_rt(cot[...], wo[...]).astype(BF16)
    for h in range(HEADS):
        qs[h, 3] = grad_attn[:, h * DH : (h + 1) * DH]

    def to_head(h, k):
        return pltpu.make_async_remote_copy(
            src_ref=qs.at[h, k], dst_ref=hb.at[k, pl.ds(pl.multiple_of(ctx * TOK, TOK), TOK), :],
            send_sem=send_sem.at[4 + k], recv_sem=recv_sem.at[14 + k],
            device_id={"dp": dp, "ctx": PLACE[h]}, device_id_type=MESH,
        )

    def to_heads(k):
        for h in range(HEADS):
            @pl.when(ctx != PLACE[h])
            def _():
                to_head(h, k).start()

    to_heads(3)

    sides_arrive(act_sides)
    edge_win = jnp.concatenate([window_matrix(-16, 16), window_matrix(ROWS, 16)], axis=1)
    sums = sums + dot(edge_win, jnp.concatenate([halo[0], halo[1]], axis=0))
    high_part = sums.astype(BF16)
    low_part = (sums - high_part.astype(F32)).astype(BF16)

    for c in range(CTX):
        cols = [high_part[j * TOK : (j + 1) * TOK, c * BLK : (c + 1) * BLK] for j in range(KW)]
        cols.append(jnp.zeros((TOK, XW - KW * BLK), BF16))
        xs[c] = jnp.concatenate(cols, axis=1)

    other = 1 - hi

    def x_send(half, c):
        return pltpu.make_async_remote_copy(
            src_ref=xs.at[c], dst_ref=xr.at[slot], send_sem=send_sem.at[10], recv_sem=recv_sem.at[5],
            device_id={"dp": zz * 2 + half, "ctx": c}, device_id_type=MESH,
        )

    @pl.loop(1, CTX)
    def _(i):
        x_send(hi, (ctx + i) % CTX).start()

    loads[6].wait()
    conv = jnp.zeros((2 * TOK, C), F32)
    for j in range(KW):
        part = slice(j * TOK, (j + 1) * TOK)
        conv = conv + dot(jnp.concatenate([high_part[part], low_part[part]], axis=0), wc[j])
    pooled = ((pooled_in + conv[:TOK] + conv[TOK:]) * (1.0 / POOL)).astype(BF16)

    for i in range(7, 10):
        loads[i].wait()
    for k, weight in ((1, wk), (0, wq), (2, wv)):
        made = dot(pooled, weight[...]).astype(BF16)
        for h in range(HEADS):
            qs[h, k] = made[:, h * DH : (h + 1) * DH]
        to_heads(k)

    def to_other_half():
        @pl.loop(0, CTX)
        def _(i):
            x_send(other, (ctx + i) % CTX).start()

        xr[slot] = xs[ctx]

    def slopes():
        @pl.loop(0, ROWS // POOL, unroll=2)
        def _(i):
            rows = pl.ds(pl.multiple_of(i * POOL, POOL), POOL)
            u = normed[rows, :] * gain_f
            square = u * u
            t = jnp.tanh(GELU_SCALE * (u + CUBIC * (square * u)))
            d = 0.5 * (1.0 + t)
            d = d + 0.5 * u * (1.0 - t * t) * GELU_SCALE * (1.0 + 3.0 * CUBIC * square)
            slope[rows, :] = d * gain_f

    def from_head(c, k):
        return pltpu.make_async_remote_copy(
            src_ref=go.at[c, k], dst_ref=gb.at[head, k],
            send_sem=send_sem.at[11], recv_sem=recv_sem.at[6],
            device_id={"dp": dp, "ctx": c}, device_id_type=MESH,
        )

    def from_heads(k):
        for dx, dy, dc in SEGMENT_FAR_FIRST:
            row = (pair // 4 + dx) % 2 * 4 + (pair + dy) % 4
            from_head(2 * row + (core + dc) % 2, k).start()

    @pl.when(is_head)
    def _():
        hb[:, pl.ds(pl.multiple_of(ctx * TOK, TOK), TOK), :] = qs[head]
        for k in range(4):
            arrived = hb.at[k, pl.ds(0, SEG_TOK - TOK), :]
            pltpu.make_async_copy(arrived, arrived, recv_sem.at[14 + k]).wait()
        scale = 1.0 / DH**0.5
        keys = hb[1]
        values = hb[2]
        values_t = values.T
        keys_t = keys.T

        @pl.loop(0, SEG_TOK // 128)
        def _(i):
            part = pl.ds(pl.multiple_of(i * 128, 128), 128)
            query = hb[0, part, :]
            grad = hb[3, part, :]
            score = dot_rt(keys, query) * scale
            expo = jnp.exp(score - jnp.max(score, axis=0, keepdims=True))
            prob = expo * (1.0 / jnp.sum(expo, axis=0, keepdims=True))
            prob_b = prob.astype(BF16)
            out_t = dot(values_t, prob_b).astype(BF16).astype(F32)
            delta = jnp.sum(grad.T.astype(F32) * out_t, axis=0, keepdims=True)
            grad_prob = dot_rt(values, grad)
            pt[:, part] = prob_b
            grad_score = (prob * (grad_prob - delta) * scale).astype(BF16)
            gst[:, part] = grad_score
            grad_query = dot(keys_t, grad_score).T.astype(BF16).reshape(4, TOK, DH)
            for m in range(4):
                go[4 * i + m, 0] = grad_query[m]
                @pl.when(ctx != 4 * i + m)
                def _():
                    from_head(4 * i + m, 0).start()

        go[:, 2] = dot(pt[...], hb[3]).astype(BF16).reshape(CTX, TOK, DH)
        from_heads(2)
        go[:, 1] = dot(gst[...], hb[0]).astype(BF16).reshape(CTX, TOK, DH)
        from_heads(1)
        to_other_half()
        gb[head] = go[ctx]
        five = gb.at[pl.ds(0, HEADS - 1)]
        pltpu.make_async_copy(five, five, recv_sem.at[6]).wait()

    @pl.when(jnp.logical_not(is_head))
    def _():
        slopes()
        to_other_half()
        pltpu.make_async_copy(gb, gb, recv_sem.at[6]).wait()

    grad_pooled = cot[...].astype(F32)
    for k, weight in enumerate((wq, wk, wv)):
        whole = jnp.concatenate([gb[h, k] for h in range(HEADS)], axis=1)
        grad_pooled = grad_pooled + dot_rt(whole, weight[...])
    grs[...] = (grad_pooled * (1.0 / POOL)).astype(BF16)
    sorted_g = dot(grs[...], perm[...]).astype(BF16)
    for k in range(PARTS):
        for h in range(2):
            first = (2 * k + h) * 128
            grp[k, h] = sorted_g[:, first : first + 128]

    for k in range(PARTS):
        for dx, dy in FAR_FIRST:
            to = (chip // 4 + dx) % 4 * 4 + (chip + dy) % 4
            pltpu.make_async_remote_copy(
                src_ref=grp.at[k, to // (CHIPS // 2)], dst_ref=grr.at[k, slot],
                send_sem=send_sem.at[12], recv_sem=recv_sem.at[7 + k],
                device_id=plane_id(2 * to + core), device_id_type=MESH,
            ).start()

        grr[k, slot] = grp[k, hi]

    row_sides = sides(grs.at[pl.ds(0, 16), :], grs.at[pl.ds(16, 16), :], grh, 2)

    @pl.when(is_head)
    def _():
        slopes()

    others = xr.at[pl.ds(0, PLANE - 1)]
    pltpu.make_async_copy(others, others, recv_sem.at[5]).wait()
    for i in range(PLANE * TOK // 128):
        block = xr[4 * i : 4 * i + 4].reshape(128, XW)
        xt[:, i * 128 : (i + 1) * 128] = block.T

    factor = 1.0 / (CTX * CTX * ROWS) ** 0.5

    def pass_on(k):
        mine = grr.at[k, pl.ds(pl.multiple_of(core * CHIPS, CHIPS), CHIPS)]
        return pltpu.make_async_remote_copy(
            src_ref=mine, dst_ref=mine, send_sem=send_sem.at[14 + k], recv_sem=recv_sem.at[11 + k],
            device_id={"dp": dp, "ctx": ctx + 1 - 2 * core}, device_id_type=MESH,
        )

    def forward(k):
        others = grr.at[k, pl.ds(0, CHIPS - 1)]
        pltpu.make_async_copy(others, others, recv_sem.at[7 + k]).wait()
        pass_on(k).start()

    def multiply(k):
        pass_on(k).wait_recv()
        made = dot(xt[...], grr[k].reshape(PLANE * TOK, 128)) * factor
        rs[k] = made.T.astype(BF16)

        for i in (4, 3, 5, 2, 6, 1, 7):
            z = (zz + i) % NZ
            pltpu.make_async_remote_copy(
                src_ref=rs.at[k, pl.ds(pl.multiple_of(z * SUB, SUB), SUB), :], dst_ref=rr.at[zz, k],
                send_sem=send_sem.at[13], recv_sem=recv_sem.at[10],
                device_id=z_id(z), device_id_type=MESH,
            ).start()

        rr[zz, k] = rs[k, pl.ds(pl.multiple_of(zz * SUB, SUB), SUB), :]

    forward(0)
    forward(1)
    multiply(0)
    forward(2)
    multiply(1)
    multiply(2)

    sides_arrive(row_sides)
    ext = jnp.concatenate([grh[0], grs[...], grh[1]], axis=0)
    first0 = first1 = mid = last0 = last1 = None
    for j in range(KW):
        y = dot_rt(ext, wc[j])
        own, before, after = y[16:48], y[15:47], y[17:49]
        terms = (
            before if j >= 3 else own,
            before if j >= 4 else own,
            own,
            after if j < 1 else own,
            after if j < 2 else own,
        )
        if j == 0:
            first0, first1, mid, last0, last1 = terms
        else:
            first0, first1, mid, last0, last1 = (
                a + b for a, b in zip((first0, first1, mid, last0, last1), terms)
            )
    for k, value in enumerate((first0, first1, mid, last0, last1, grs[...].astype(F32))):
        edge[k] = value

    in_group = lax.broadcasted_iota(jnp.int32, (POOL, C), 0)

    @pl.loop(0, TOK, unroll=2)
    def _(i):
        rows = pl.ds(pl.multiple_of(i * POOL, POOL), POOL)
        one = pl.ds(i, 1)
        g = jnp.broadcast_to(edge[2, one, :], (POOL, C))
        for r, k in ((0, 0), (1, 1), (14, 3), (15, 4)):
            g = jnp.where(in_group == r, edge[k, one, :], g)
        g = g * slope[rows, :]
        n = normed[rows, :]
        mean = jnp.mean(g * n, axis=-1, keepdims=True)
        grad_in_ref[rows, :] = (edge[5, one, :] + inv[rows, :] * (g - n * mean)).astype(BF16)

    grad_in_out = pltpu.make_async_copy(grad_in_ref, grad_in_h, in_sem.at[10])
    grad_in_out.start()

    others = rr.at[pl.ds(0, NZ - 1)]
    pltpu.make_async_copy(others, others, recv_sem.at[10]).wait()
    total = rr[0].astype(F32)
    for z in range(1, NZ):
        total = total + rr[z].astype(F32)
    total = jnp.concatenate([total.reshape(BLK, XW), jnp.zeros((128 - BLK, XW), F32)], axis=0).T
    for j in range(KW):
        grad_conv_ref[j] = total[j * BLK : (j + 1) * BLK, :BLK]

    grad_in_out.wait()
    sides_sent(act_sides)
    sides_sent(row_sides)
    for k in range(4):
        @pl.when(is_head)
        def _():
            part = qs.at[pl.ds(0, HEADS - 1), k]
            pltpu.make_async_copy(part, part, send_sem.at[4 + k]).wait()

        @pl.when(jnp.logical_not(is_head))
        def _():
            part = qs.at[:, k]
            pltpu.make_async_copy(part, part, send_sem.at[4 + k]).wait()
    part = xr.at[pl.ds(0, PLANE - 1)]
    pltpu.make_async_copy(part, part, send_sem.at[10]).wait()

    @pl.when(is_head)
    def _():
        part = go.at[pl.ds(0, CTX - 1)]
        pltpu.make_async_copy(part, part, send_sem.at[11]).wait()

    part = grr.at[:, pl.ds(0, CHIPS - 1)]
    pltpu.make_async_copy(part, part, send_sem.at[12]).wait()
    for k in range(PARTS):
        pass_on(k).wait_send()
    part = rr.at[pl.ds(0, NZ - 1)]
    pltpu.make_async_copy(part, part, send_sem.at[13]).wait()


def write_out(grad_in_h, grad_conv_h, grad_in_o, grad_conv_o, rows_v, conv_v, in_sem, out_sem):
    step = ROWS // COPIES
    pieces = [pl.ds(i * step, step) for i in range(COPIES)]
    steps = [
        (
            pltpu.make_async_copy(grad_in_h.at[rows, :], rows_v.at[rows, :], in_sem.at[i]),
            pltpu.make_async_copy(rows_v.at[rows, :], grad_in_o.at[rows, :], out_sem.at[i]),
        )
        for i, rows in enumerate(pieces)
    ]
    steps.append(
        (
            pltpu.make_async_copy(grad_conv_h, conv_v, in_sem.at[COPIES]),
            pltpu.make_async_copy(conv_v, grad_conv_o, out_sem.at[COPIES]),
        )
    )
    for load, _ in steps:
        load.start()
    for load, store in steps:
        load.wait()
        store.start()
    for _, store in steps:
        store.wait()


def per_device(
    features, bases, dna_table, norm_gain, w_conv, w_query, w_key, w_value, w_out, cotangent
):
    vmem = pltpu.VMEM
    scratch = [
        vmem((ROWS, C), BF16), vmem((1, ROWS), jnp.int32), vmem((4, C), BF16), vmem((C,), BF16),
        vmem((KW, C, C), BF16), vmem((C, C), BF16), vmem((C, C), BF16), vmem((C, C), BF16),
        vmem((C, C), BF16), vmem((TOK, C), BF16),
        vmem((ROWS, C), BF16),
        vmem((ROWS, C), BF16),
        vmem((ROWS, C), F32),
        vmem((ROWS, 1), F32),
        vmem((ROWS, C), F32),
        vmem((KW * TOK, ROWS), BF16),
        vmem((2, 16, C), BF16),
        vmem((CTX, TOK, XW), BF16),
        vmem((PLANE, TOK, XW), BF16),
        vmem((XW, PLANE * TOK), BF16),
        vmem((HEADS, 4, TOK, DH), BF16),
        vmem((4, SEG_TOK, DH), BF16),
        vmem((SEG_TOK, SEG_TOK), BF16),
        vmem((SEG_TOK, SEG_TOK), BF16),
        vmem((CTX, 3, TOK, DH), BF16),
        vmem((HEADS, 3, TOK, DH), BF16),
        vmem((C, C), BF16),
        vmem((PARTS, 2, TOK, 128), BF16),
        vmem((PARTS, PLANE, TOK, 128), BF16),
        vmem((2, 16, C), BF16),
        vmem((TOK, C), BF16),
        vmem((PARTS, 128, XW), BF16),
        vmem((NZ, PARTS, SUB, XW), BF16),
        vmem((6, TOK, C), F32),
        vmem((ROWS, C), BF16),
        pltpu.SemaphoreType.DMA((11,)),
        pltpu.SemaphoreType.DMA((17,)),
        pltpu.SemaphoreType.DMA((18,)),
    ]
    grad_in, grad_conv = pl.pallas_call(
        body,
        out_shape=(
            jax.ShapeDtypeStruct((ROWS, C), BF16),
            jax.ShapeDtypeStruct((KW, BLK, BLK), F32),
        ),
        in_specs=[pl.BlockSpec(memory_space=pltpu.HBM)] * 10,
        out_specs=(pl.BlockSpec(memory_space=pltpu.HBM), pl.BlockSpec(memory_space=pltpu.VMEM)),
        scratch_shapes=scratch,
        compiler_params=pltpu.CompilerParams(
            collective_id=0, has_side_effects=True, vmem_limit_bytes=56 * 1024 * 1024
        ),
        cost_estimate=pl.CostEstimate(flops=10**9, bytes_accessed=12 * 10**6, transcendentals=10**6),
    )(
        features[0], bases, dna_table, norm_gain, w_conv, w_query, w_key, w_value, w_out,
        cotangent[0],
    )
    grad_in, grad_conv = pl.pallas_call(
        write_out,
        out_shape=(
            jax.ShapeDtypeStruct((ROWS, C), BF16),
            jax.ShapeDtypeStruct((KW, BLK, BLK), F32),
        ),
        in_specs=[pl.BlockSpec(memory_space=pltpu.HBM)] * 2,
        out_specs=(pl.BlockSpec(memory_space=pltpu.HBM),) * 2,
        scratch_shapes=[
            vmem((ROWS, C), BF16), vmem((KW, BLK, BLK), F32),
            pltpu.SemaphoreType.DMA((COPIES + 1,)), pltpu.SemaphoreType.DMA((COPIES + 1,)),
        ],
        compiler_params=pltpu.CompilerParams(vmem_limit_bytes=56 * 1024 * 1024),
    )(grad_in, grad_conv)
    return grad_in[None], grad_conv.transpose(1, 0, 2)


def solution(mesh):
    in_specs = (
        P("dp", "ctx", None),
        P("dp", "ctx"),
        P(),
        P(),
        P(),
        P(),
        P(),
        P(),
        P(),
        P("dp", "ctx", None),
    )
    out_specs = (P("dp", "ctx", None), P("ctx", None, "dp"))
    return jax.shard_map(
        per_device, mesh=mesh, in_specs=in_specs, out_specs=out_specs, check_vma=False
    )
```
